256 devices in a mesh: video: 16 (over z, core), tm: 4 (over x), height: 4 (over y).
Axes of the slice: x: 4, y: 4, z: 8, core: 2. Of those that a mesh axis runs over, the one named last changes fastest.
Arguments:
- features: bfloat16 [16, 2, 32, 96, 8, 128], P('video', None, 'tm', None, 'height'), may hold values from -6 to 6
- frame_counts: int32 [16], replicated, may hold values from 31 to 64, as said below
- places: int32 [16, 32], replicated, may hold values from 0 to 320, as said below
- gain_one: float32 [96], replicated, may hold values from 0.5 to 2
- gain_two: float32 [96], replicated, may hold values from 0.5 to 2
- conv_one: bfloat16 [3, 3, 3, 96, 96], replicated, may hold values from -0.375 to 0.375
- conv_two: bfloat16 [3, 3, 3, 96, 96], replicated, may hold values from -0.375 to 0.375
- bias_one: float32 [96], replicated, may hold values from -3 to 3
- bias_two: float32 [96], replicated, may hold values from -3 to 3
Outputs:
- scored_frames: bfloat16 [16, 40, 96, 8, 128], P('video', 'tm', None, 'height')
The draws below stay inside these ranges and needn't reach their ends.
Inputs may be any that keep to these rules, and one draw needn't show every extreme that they name: Video v has ceil(frame_counts[v] / 2) live blocks (blocks g with 2 g < frame_counts[v]), a multiple of 16; together the videos have exactly 272 live blocks. `places`: block g lies on tm index (g // 4) % 4. A live block holds a place below 320, no two live blocks the same; a block that is not live holds 320. Owner o is the device of video index o // 4 and tm index o % 4; a live block goes to an owner of its own tm index. Of the 8 blocks of one video on one tm index, at most 1 live ones have one owner p // 5.
All inputs are finite; a program needn't handle non-finite values.
Results may differ from the reference program's by a relative error of at most 0.008.
Values may be sent and summed in bfloat16 or wider, within the bound.
No kernel may reach another device: no remote copies, remote signals or barrier semaphores. Data moves between devices by JAX's collectives and lax.ppermute only.
A program may use at most 128 MiB of HBM per device.

```python
import math
import jax
import jax.numpy as jnp
from jax import lax

C = 96
W = 128
BF = 2
RB = 4
ROUNDS = 2
UNIT = 16
VIDEOS = 16
BLOCKS = 32
FRAMES = 64
ROWS = 8
OWNERS = 64
LIVE = 272
SLOTS = 5
N_TM = 4


def block_units(key):
    longest = jax.random.randint(jax.random.fold_in(key, 101), (), 0, VIDEOS)
    leanings = jax.random.randint(jax.random.fold_in(key, 102), (VIDEOS,), 1, 5)
    video_ids = jnp.arange(VIDEOS)
    start_units = jnp.where(video_ids == longest, ROUNDS, 1).astype(jnp.int32)

    def add_unit(step, units_now):
        picks = jax.random.randint(jax.random.fold_in(key, 1000 + step), (VIDEOS,), 0, 65536)
        scores = picks * leanings * VIDEOS + video_ids
        scores = jnp.where((units_now < ROUNDS - 1) & (video_ids != longest), scores, -1)
        chosen = jnp.argmax(scores)
        return units_now + (video_ids == chosen).astype(jnp.int32)
    units = lax.fori_loop(0, LIVE // UNIT - ROUNDS - VIDEOS + 1, add_unit, start_units)
    return (units, longest)


def draw_frame_counts(key, part):
    units, longest = block_units(key)
    key = jax.random.fold_in(key, 7)
    shorten = jax.random.randint(key, (VIDEOS,), 0, BF)
    shorten = jnp.where(jnp.arange(VIDEOS) == longest, 0, shorten)
    return (units * UNIT * BF - shorten).astype(jnp.int32)


def draw_places(key, part):
    units, longest = block_units(key)
    key = jax.random.fold_in(key, 9)
    tm_count = UNIT // RB
    live = (jnp.arange(BLOCKS)[None, :] < (units * UNIT)[:, None]).astype(jnp.int32)
    by_tm = live.reshape(VIDEOS, ROUNDS, tm_count, RB).transpose(2, 0, 1, 3).reshape(tm_count, VIDEOS * ROUNDS * RB)
    ranks = jnp.cumsum(by_tm, axis=1) - by_tm
    orders = jax.vmap(lambda sub_key: jax.random.permutation(sub_key, VIDEOS))(jax.random.split(key, tm_count))
    owner_video = jnp.take_along_axis(orders, ranks % VIDEOS, axis=1)
    tm_ids = jnp.arange(tm_count)[:, None]
    spots = (owner_video * tm_count + tm_ids) * SLOTS + ranks // VIDEOS
    spots = jnp.where(by_tm == 1, spots, OWNERS * SLOTS)
    back = spots.reshape(tm_count, VIDEOS, ROUNDS, RB).transpose(1, 2, 0, 3).reshape(VIDEOS, BLOCKS)
    return back.astype(jnp.int32)


def steps_of(stream_key, shape, shards, low, high):
    gain = 1.0
    for dim, parts in shards:
        heights = jax.random.uniform(jax.random.fold_in(jax.random.fold_in(stream_key, 6), dim), (parts,), jnp.float32, low / len(shards), high / len(shards))
        gain = gain * jnp.repeat(jnp.exp(heights), shape[dim] // parts).reshape((-1,) + (1,) * (len(shape) - 1 - dim))
    return gain


def normal_values(rng, shape, spread, reach, cuts=(), kind=jnp.bfloat16):
    entries = spread * jax.random.normal(rng, shape, jnp.float32)
    if cuts:
        entries = entries * steps_of(rng, shape, cuts, -0.22, 0.18)
    return jnp.clip(entries, -reach, reach).astype(kind)


def setup_inputs(seed: int = 0) -> dict:
    arg_keys = jax.random.split(jax.random.key(seed), 10)
    return {
        "features": normal_values(arg_keys[0], (VIDEOS, ROUNDS, UNIT * BF, C, ROWS, W), 1.0, 6.0, ((0, 16), (2, 4), (4, 4))),
        "frame_counts": draw_frame_counts(jax.random.fold_in(arg_keys[9], 71), 0),
        "places": draw_places(jax.random.fold_in(arg_keys[9], 71), 0),
        "gain_one": jnp.clip(jnp.exp(jax.random.uniform(arg_keys[3], (C,), jnp.float32, math.log(0.5), math.log(2.0))), 0.5, 2.0),
        "gain_two": jnp.clip(jnp.exp(jax.random.uniform(arg_keys[4], (C,), jnp.float32, math.log(0.5), math.log(2.0))), 0.5, 2.0),
        "conv_one": normal_values(arg_keys[5], (3, 3, 3, C, C), (3 * C) ** -0.5, 0.375),
        "conv_two": normal_values(arg_keys[6], (3, 3, 3, C, C), (3 * C) ** -0.5, 0.375),
        "bias_one": normal_values(arg_keys[7], (C,), 0.5, 3.0, (), jnp.float32),
        "bias_two": normal_values(arg_keys[8], (C,), 0.5, 3.0, (), jnp.float32),
    }


EPS = 1e-06

def activate(values, scales):
    values = values.astype(jnp.float32)
    mean_square = lax.optimization_barrier(jnp.mean(values * values, axis=1, keepdims=True))
    scaled = values * lax.rsqrt(mean_square + EPS) * scales[None, :, None, None]
    return jax.nn.silu(scaled).astype(jnp.bfloat16)

def convolve(inputs, weight, offset):
    frame_count = inputs.shape[0]
    row_count = inputs.shape[2]
    cell_count = inputs.shape[3]
    padded = jnp.pad(inputs.astype(jnp.float32), ((2, 0), (0, 0), (1, 1), (1, 1)))
    kernel = weight.astype(jnp.float32)
    summed = jnp.zeros((frame_count, weight.shape[3], row_count, cell_count), jnp.float32)
    for tap_time in range(3):
        for tap_row in range(3):
            for tap_cell in range(3):
                window = padded[tap_time:tap_time + frame_count, :, tap_row:tap_row + row_count, tap_cell:tap_cell + cell_count]
                summed = summed + jnp.einsum('oc,fchw->fohw', kernel[tap_time, tap_row, tap_cell], window)
    return summed + offset[None, :, None, None]

def reference(features, frame_counts, places, gain_one, gain_two, conv_one, conv_two, bias_one, bias_two):
    clips = features.reshape(VIDEOS, FRAMES, C, ROWS, W)

    def decode_video(video_pair):
        clip_frames, frame_limit = video_pair
        first_act = activate(clip_frames, gain_one)
        middle = convolve(first_act, conv_one, bias_one).astype(jnp.bfloat16)
        second = activate(middle, gain_two)
        result = clip_frames.astype(jnp.float32) + convolve(second, conv_two, bias_two)
        in_range = (jnp.arange(FRAMES) < frame_limit).astype(jnp.float32)
        return (result * in_range[:, None, None, None]).astype(jnp.bfloat16)
    decoded = lax.map(decode_video, (clips, frame_counts))
    blocks_all = decoded.reshape(VIDEOS * BLOCKS, BF, C, ROWS, W)
    holder = jnp.zeros((OWNERS * SLOTS + 1, BF, C, ROWS, W), jnp.bfloat16)
    holder = holder.at[places.reshape(-1).astype(jnp.int32)].set(blocks_all)
    return holder[:OWNERS * SLOTS].reshape(VIDEOS, N_TM * SLOTS * BF, C, ROWS, W)
```

```python
import functools

import jax
import jax.numpy as jnp
from jax import lax
from jax.experimental import pallas as pl
from jax.experimental.pallas import tpu as pltpu
from jax.sharding import PartitionSpec as P

EPS = 1e-06
BF = 2
RB = 4
SEG = BF * RB
TAIL = 2 * BF
C = 96
W = 128
TAPS = 3 * C
SLOTS = 5


def activate(values, gain, axis):
    mean_square = jnp.mean(values * values, axis=axis, keepdims=True)
    scaled = values * lax.rsqrt(mean_square + EPS) * gain
    return scaled * (0.5 * jnp.tanh(0.5 * scaled) + 0.5)


def ring(value, axis):
    count = lax.axis_size(axis)
    return lax.ppermute(value, axis, [(i, (i + 1) % count) for i in range(count)])


def neighbours(value, axis):
    up = [(i, i + 1) for i in range(lax.axis_size(axis) - 1)]
    return (
        lax.ppermute(value, axis, up),
        lax.ppermute(value, axis, [(target, source) for source, target in up]),
    )


def spread(values, stack, row, frame):
    lane = lax.broadcasted_iota(jnp.int32, values.shape, 1)
    left = jnp.where(lane == 0, 0.0, pltpu.roll(values, 1, 1))
    right = jnp.where(lane == W - 1, 0.0, pltpu.roll(values, W - 1, 1))
    columns = slice(frame * W, (frame + 1) * W)
    for tap, shifted in enumerate((left, values, right)):
        start = row * TAPS + tap * C
        stack[start : start + C, columns] = shifted.astype(jnp.bfloat16)


def multiply(weights, stack, row, frame, frames):
    total = None
    for tap in range(3):
        window = stack[
            row * TAPS : (row + 4) * TAPS, (frame + tap) * W : (frame + tap + frames) * W
        ]
        part = jnp.dot(weights[tap], window, preferred_element_type=jnp.float32)
        total = part if total is None else total + part
    return total


def decode_kernel(
    flags,
    raw,
    own,
    low,
    high,
    tail,
    low_tail,
    high_tail,
    weights_one,
    weights_two,
    gain_two,
    bias_one,
    bias_two,
    boxes,
    first,
    second,
):
    turn = pl.program_id(0)

    @pl.when(flags[turn] > 0)
    def _():
        has_past = flags[2 + turn] > 0
        above = flags[4] > 0
        below = flags[5] > 0
        limit = flags[6 + turn]
        for frame in range(TAIL):
            for row in range(6):
                source = (low_tail, tail, high_tail)[row // 2]
                values = source[0, frame, row % 2].astype(jnp.float32)
                spread(jnp.where(has_past, values, 0.0), first, row, frame)
        for frame in range(SEG):
            for row in range(6):
                source = (low, own, high)[row // 2]
                spread(source[0, frame, row % 2].astype(jnp.float32), first, row, TAIL + frame)
        gain = gain_two[...]
        offset = bias_one[...]
        for row in range(0, 4, 2):
            for frame in range(0, SEG + 2, 2):
                total = multiply(weights_one, first, row, frame, 2)
                for k in range(2):
                    for j in range(2):
                        part = total[k * C : (k + 1) * C, j * W : (j + 1) * W] + offset
                        part = part.astype(jnp.bfloat16).astype(jnp.float32)
                        part = activate(part, gain, 0)
                        keep = None
                        if frame < 2:
                            keep = has_past
                        if row + k == 0:
                            keep = above if keep is None else jnp.logical_and(keep, above)
                        if row + k == 3:
                            keep = below if keep is None else jnp.logical_and(keep, below)
                        if keep is not None:
                            part = jnp.where(keep, part, 0.0)
                        spread(part, second, row + k, frame + j)
        offset = bias_two[...]
        for block in range(RB):
            target = flags[8 + turn * RB + block]
            total = multiply(weights_two, second, 0, block * BF, BF)
            for k in range(2):
                for j in range(BF):
                    frame = block * BF + j
                    part = total[k * C : (k + 1) * C, j * W : (j + 1) * W] + offset
                    part = part + raw[0, frame, k].astype(jnp.float32)
                    part = jnp.where(frame < limit, part, 0.0)
                    boxes[target, j, k] = part.astype(jnp.bfloat16)


def decode(flags, raw, own, sides, tail, tail_sides, weights, gain_two, biases, box_count):
    rounds = raw.shape[0]

    def whole(array):
        return pl.BlockSpec(array.shape, lambda r, flags: (0,) * array.ndim)

    def by_round(array):
        return pl.BlockSpec((1,) + array.shape[1:], lambda r, flags: (r, 0, 0, 0, 0))

    def by_source(array):
        return pl.BlockSpec((1,) + array.shape[1:], lambda r, flags: (flags[16 + r], 0, 0, 0, 0))

    constants = (*weights, gain_two, *biases)
    box_shape = (box_count, BF, 2, C, W)
    return pl.pallas_call(
        decode_kernel,
        out_shape=jax.ShapeDtypeStruct(box_shape, jnp.bfloat16),
        grid_spec=pltpu.PrefetchScalarGridSpec(
            num_scalar_prefetch=1,
            grid=(rounds,),
            in_specs=[
                by_round(raw),
                by_round(own),
                by_round(sides[0]),
                by_round(sides[1]),
                by_source(tail),
                by_source(tail_sides[0]),
                by_source(tail_sides[1]),
                *[whole(array) for array in constants],
            ],
            out_specs=pl.BlockSpec(box_shape, lambda r, flags: (0, 0, 0, 0, 0)),
            scratch_shapes=[
                pltpu.VMEM((6 * TAPS, (TAIL + SEG) * W), jnp.bfloat16),
                pltpu.VMEM((4 * TAPS, (2 + SEG) * W), jnp.bfloat16),
            ],
        ),
        compiler_params=pltpu.CompilerParams(vmem_limit_bytes=48 * 2**20),
        name="decode",
    )(flags, raw, own, *sides, tail, *tail_sides, *constants)


def pair_weights(weight):
    base = jnp.transpose(weight, (0, 3, 1, 2, 4))
    upper = jnp.pad(base, ((0, 0), (0, 0), (0, 1), (0, 0), (0, 0)))
    lower = jnp.pad(base, ((0, 0), (0, 0), (1, 0), (0, 0), (0, 0)))
    return jnp.stack([upper, lower], axis=1).reshape(3, 2 * C, 4 * TAPS)


def local(
    features, frame_counts, places, gain_one, gain_two, conv_one, conv_two, bias_one, bias_two
):
    my_video = lax.axis_index("video")
    my_tm = lax.axis_index("tm")
    my_height = lax.axis_index("height")
    videos = lax.axis_size("video")
    tm_count = lax.axis_size("tm")
    heights = lax.axis_size("height")
    rounds = features.shape[1]

    raw = jnp.swapaxes(features[0], 2, 3)
    own = activate(raw.astype(jnp.float32), gain_one[:, None], 3).astype(jnp.bfloat16)
    tail = ring(own[:, SEG - TAIL :], "tm")
    sides = neighbours(own, "height")
    tail_sides = neighbours(tail, "height")

    held = lax.dynamic_index_in_dim(
        places.reshape(videos, rounds, tm_count, RB), my_tm, 2, keepdims=False
    )
    mine = lax.dynamic_index_in_dim(held, my_video, 0, keepdims=False)
    turns = jnp.arange(rounds)
    count = lax.dynamic_index_in_dim(frame_counts, my_video, 0, keepdims=False)
    start = (turns * tm_count + my_tm) * SEG
    live = (count > turns * tm_count * SEG).astype(jnp.int32)
    past = jnp.logical_or(turns > 0, my_tm > 0).astype(jnp.int32)
    edges = jnp.stack([my_height > 0, my_height < heights - 1]).astype(jnp.int32)
    owner = jnp.minimum(mine // (SLOTS * tm_count), videos - 1)
    tail_round = jnp.where(my_tm == 0, jnp.maximum(turns - 1, 0), turns)
    flags = jnp.concatenate(
        [live, past, edges, count - start, owner.reshape(-1), tail_round]
    ).astype(jnp.int32)

    weights = (pair_weights(conv_one), pair_weights(conv_two))
    wide = [jnp.broadcast_to(v[:, None], (C, W)) for v in (gain_two, bias_one, bias_two)]
    boxes = decode(
        flags, raw, own, sides, tail, tail_sides, weights, wide[0], wide[1:], videos
    )
    received = lax.all_to_all(boxes, "video", split_axis=0, concat_axis=0, tiled=True)

    wanted = (my_video * tm_count + my_tm) * SLOTS + jnp.arange(SLOTS)
    match = (held.reshape(videos, -1)[None] == wanted[:, None, None]).astype(jnp.int32)
    found = jnp.sum(match, axis=(1, 2)) > 0
    source = jnp.sum(match * jnp.arange(videos)[None, :, None], axis=(1, 2))
    chosen = jnp.stack(
        [
            jnp.where(
                found[k],
                lax.dynamic_index_in_dim(received, source[k], 0, keepdims=False),
                jnp.zeros((), jnp.bfloat16),
            )
            for k in range(SLOTS)
        ]
    )
    return jnp.swapaxes(chosen, 2, 3).reshape(1, SLOTS * BF, C, 2, W)


def solution(mesh):
    placed = (P("video", None, "tm", None, "height", None), P(), P(), P(), P(), P(), P(), P(), P())
    return jax.shard_map(
        local,
        mesh=mesh,
        in_specs=placed,
        out_specs=P("video", "tm", None, "height", None),
        check_vma=False,
    )
```

```python
import functools

import jax
import jax.numpy as jnp
from jax import lax
from jax.experimental import pallas as pl
from jax.experimental.pallas import tpu as pltpu
from jax.sharding import PartitionSpec as P

EPS = 1e-06
BF = 2
RB = 4
SEG = BF * RB
TAIL = 2 * BF
C = 96
W = 128
TAPS = 3 * C
SLOTS = 5


def activate(values, gain, axis):
    mean_square = jnp.mean(values * values, axis=axis, keepdims=True)
    scaled = values * lax.rsqrt(mean_square + EPS) * gain
    return scaled * (0.5 * jnp.tanh(0.5 * scaled) + 0.5)


def ring(value, axis):
    count = lax.axis_size(axis)
    return lax.ppermute(value, axis, [(i, (i + 1) % count) for i in range(count)])


def neighbours(value, axis):
    up = [(i, i + 1) for i in range(lax.axis_size(axis) - 1)]
    return (
        lax.ppermute(value, axis, up),
        lax.ppermute(value, axis, [(target, source) for source, target in up]),
    )


def spread(values, stack, row, columns):
    lane = lax.broadcasted_iota(jnp.int32, values.shape, 1)
    left = jnp.where(lane == 0, 0.0, pltpu.roll(values, 1, 1))
    right = jnp.where(lane == W - 1, 0.0, pltpu.roll(values, W - 1, 1))
    for tap, shifted in enumerate((left, values, right)):
        start = row * TAPS + tap * C
        stack[start : start + C, columns] = shifted.astype(jnp.bfloat16)


def cells(frame, frames=1):
    return pl.ds(pl.multiple_of(frame * W, W), frames * W)


def multiply(weights, stack, row, frame):
    total = None
    for tap in range(3):
        window = stack[row * TAPS : (row + 4) * TAPS, cells(frame + tap, 2)]
        part = jnp.dot(weights[tap], window, preferred_element_type=jnp.float32)
        total = part if total is None else total + part
    return total


def decode_kernel(
    flags,
    raw,
    own,
    low,
    high,
    tail,
    low_tail,
    high_tail,
    weights_one,
    weights_two,
    gain_two,
    bias_one,
    bias_two,
    *rest,
):
    boxes, first, second = rest[-3:]
    step = pl.program_id(0)
    live = flags[0] > 0

    @pl.when(jnp.logical_and(live, step == 0))
    def _():
        for frame in range(TAIL):
            for row in range(6):
                source = (low_tail, tail, high_tail)[row // 2]
                spread(source[frame, row % 2].astype(jnp.float32), first, row, cells(frame))

    @pl.when(jnp.logical_and(live, step > 0))
    def _():
        for j in range(2):
            for row in range(6):
                source = (low, own, high)[row // 2]
                values = source[(step - 1) * 2 + j, row % 2].astype(jnp.float32)
                spread(values, first, row, cells(step * 2 + 2 + j))

    @pl.when(live)
    def _():
        past = jnp.logical_or(flags[1] > 0, step > 0)
        keeps = (
            jnp.logical_and(past, flags[2] > 0),
            past,
            past,
            jnp.logical_and(past, flags[3] > 0),
        )
        gain = gain_two[...]
        offset = bias_one[...]
        for row in range(0, 4, 2):
            total = multiply(weights_one, first, row, step * 2)
            for k in range(2):
                for j in range(2):
                    part = total[k * C : (k + 1) * C, j * W : (j + 1) * W] + offset
                    part = part.astype(jnp.bfloat16).astype(jnp.float32)
                    part = jnp.where(keeps[row + k], activate(part, gain, 0), 0.0)
                    spread(part, second, row + k, cells(step * 2 + j))

    @pl.when(jnp.logical_and(live, step > 0))
    def _():
        offset = bias_two[...]
        total = multiply(weights_two, second, 0, (step - 1) * 2)
        for j in range(BF):
            frame = (step - 1) * BF + j
            for k in range(2):
                part = total[k * C : (k + 1) * C, j * W : (j + 1) * W] + offset
                part = part + raw[frame, k].astype(jnp.float32)
                part = jnp.where(frame < flags[4], part, 0.0)
                boxes[0, j, k] = part.astype(jnp.bfloat16)


def decode(flags, raw, own, sides, tail, tail_sides, constants, boxes, box_count):
    def part(frames, place):
        return pl.BlockSpec((frames, 2, C, W), lambda p, flags: (place, 0, 0, 0))

    def whole(array):
        return pl.BlockSpec(array.shape, lambda p, flags: (0,) * array.ndim)

    joined = tail_sides is None
    tail_part = part(TAIL, SEG // TAIL if joined else 0)
    operands = [flags, raw, own, *sides, tail, *(sides if joined else tail_sides), *constants]
    specs = [part(SEG, 0)] * 4 + [part(TAIL, 0), tail_part, tail_part]
    specs += [whole(array) for array in constants]
    aliases = {}
    if boxes is not None:
        aliases = {len(operands): 0}
        operands.append(boxes)
        specs.append(pl.BlockSpec(memory_space=pl.ANY))
    return pl.pallas_call(
        decode_kernel,
        out_shape=jax.ShapeDtypeStruct((box_count, BF, 2, C, W), jnp.bfloat16),
        grid_spec=pltpu.PrefetchScalarGridSpec(
            num_scalar_prefetch=1,
            grid=(RB + 1,),
            in_specs=specs,
            out_specs=pl.BlockSpec(
                (1, BF, 2, C, W),
                lambda p, flags: (flags[5 + jnp.maximum(p - 1, 0)], 0, 0, 0, 0),
            ),
            scratch_shapes=[
                pltpu.VMEM((6 * TAPS, (TAIL + SEG) * W), jnp.bfloat16),
                pltpu.VMEM((4 * TAPS, (2 + SEG) * W), jnp.bfloat16),
            ],
        ),
        input_output_aliases=aliases,
        compiler_params=pltpu.CompilerParams(vmem_limit_bytes=40 * 2**20),
        cost_estimate=pl.CostEstimate(flops=6 * 10**9, bytes_accessed=4 * 10**6, transcendentals=0),
        name="decode",
    )(*operands)


def pair_kernel(one, two, pair_one, pair_two):
    for weight, pair in ((one, pair_one), (two, pair_two)):
        pair[...] = jnp.zeros(pair.shape, pair.dtype)
        for tap in range(3):
            for row in range(3):
                for cell in range(3):
                    tile = weight[tap, row, cell]
                    for k in range(2):
                        start = ((row + k) * 3 + cell) * C
                        pair[tap, k * C : (k + 1) * C, start : start + C] = tile


def pair_weights(one, two):
    shape = jax.ShapeDtypeStruct((3, 2 * C, 4 * TAPS), jnp.bfloat16)
    return pl.pallas_call(
        pair_kernel,
        out_shape=(shape, shape),
        in_specs=[pl.BlockSpec(memory_space=pltpu.VMEM)] * 2,
        out_specs=[pl.BlockSpec(memory_space=pltpu.VMEM)] * 2,
        compiler_params=pltpu.CompilerParams(vmem_limit_bytes=32 * 2**20),
        name="pair_weights",
    )(one, two)


def pick_kernel(picks, received, chosen):
    k = pl.program_id(0)

    @pl.when(picks[SLOTS + k] > 0)
    def _():
        for frame in range(BF):
            chosen[frame] = jnp.swapaxes(received[0, frame], 0, 1)

    @pl.when(picks[SLOTS + k] == 0)
    def _():
        chosen[...] = jnp.zeros(chosen.shape, chosen.dtype)


def pick(picks, received):
    return pl.pallas_call(
        pick_kernel,
        out_shape=jax.ShapeDtypeStruct((SLOTS * BF, C, 2, W), jnp.bfloat16),
        grid_spec=pltpu.PrefetchScalarGridSpec(
            num_scalar_prefetch=1,
            grid=(SLOTS,),
            in_specs=[
                pl.BlockSpec((1, BF, 2, C, W), lambda k, picks: (picks[k], 0, 0, 0, 0))
            ],
            out_specs=pl.BlockSpec((BF, C, 2, W), lambda k, picks: (k, 0, 0, 0)),
        ),
        name="pick",
    )(picks, received)


def local(
    features, frame_counts, places, gain_one, gain_two, conv_one, conv_two, bias_one, bias_two
):
    my_video = lax.axis_index("video")
    my_tm = lax.axis_index("tm")
    my_height = lax.axis_index("height")
    videos = lax.axis_size("video")
    tm_count = lax.axis_size("tm")
    heights = lax.axis_size("height")
    rounds = features.shape[1]

    raw = jnp.swapaxes(features[0], 2, 3)
    own = activate(raw.astype(jnp.float32), gain_one[:, None], 3).astype(jnp.bfloat16)
    tails = ring(own[:, SEG - TAIL :], "tm")
    leads = my_tm == 0
    tail_0 = jnp.where(leads, jnp.zeros((), jnp.bfloat16), tails[0])
    tail_1 = jnp.where(leads, tails[0], tails[1])
    sides_0 = neighbours(own[0], "height")
    tail_sides_0 = neighbours(tail_0, "height")
    sides_1 = neighbours(jnp.concatenate([own[1], tail_1]), "height")

    held = lax.dynamic_index_in_dim(
        places.reshape(videos, rounds, tm_count, RB), my_tm, 2, keepdims=False
    )
    mine = lax.dynamic_index_in_dim(held, my_video, 0, keepdims=False)
    count = lax.dynamic_index_in_dim(frame_counts, my_video, 0, keepdims=False)
    owner = mine // (SLOTS * tm_count)
    used = jnp.any(owner[0][None, :] == jnp.arange(videos)[:, None], axis=1)
    spare = jnp.argmin(used)
    flags = []
    for turn in range(rounds):
        live = count > turn * tm_count * SEG
        past = jnp.logical_or(turn > 0, my_tm > 0)
        limit = count - (turn * tm_count + my_tm) * SEG
        head = jnp.stack([live, past, my_height > 0, my_height < heights - 1, limit])
        flags.append(jnp.concatenate([head, jnp.where(live, owner[turn], spare)]).astype(jnp.int32))

    wide = [jnp.broadcast_to(v[:, None], (C, W)) for v in (gain_two, bias_one, bias_two)]
    constants = (*pair_weights(conv_one, conv_two), *wide)
    boxes = decode(
        flags[0], raw[0], own[0], sides_0, tail_0, tail_sides_0, constants, None, videos
    )
    boxes = decode(flags[1], raw[1], own[1], sides_1, tail_1, None, constants, boxes, videos)
    received = lax.all_to_all(boxes, "video", split_axis=0, concat_axis=0, tiled=True)

    wanted = (my_video * tm_count + my_tm) * SLOTS + jnp.arange(SLOTS)
    match = (held.reshape(videos, -1)[None] == wanted[:, None, None]).astype(jnp.int32)
    found = jnp.sum(match, axis=(1, 2))
    source = jnp.sum(match * jnp.arange(videos)[None, :, None], axis=(1, 2))
    picks = jnp.concatenate([source, found]).astype(jnp.int32)
    return pick(picks, received).reshape(1, SLOTS * BF, C, 2, W)


def solution(mesh):
    placed = (P("video", None, "tm", None, "height", None), P(), P(), P(), P(), P(), P(), P(), P())
    return jax.shard_map(
        local,
        mesh=mesh,
        in_specs=placed,
        out_specs=P("video", "tm", None, "height", None),
        check_vma=False,
    )
```

```python
import functools

import jax
import jax.numpy as jnp
from jax import lax
from jax.experimental import pallas as pl
from jax.experimental.pallas import tpu as pltpu
from jax.sharding import PartitionSpec as P

EPS = 1e-06
BF = 2
RB = 4
SEG = BF * RB
TAIL = 2 * BF
C = 96
W = 128
TAPS = 3 * C
SLOTS = 5


def activate(values, gain, axis):
    mean_square = jnp.mean(values * values, axis=axis, keepdims=True)
    scaled = values * lax.rsqrt(mean_square + EPS) * gain
    return scaled * (0.5 * jnp.tanh(0.5 * scaled) + 0.5)


def ring(value, axis):
    count = lax.axis_size(axis)
    return lax.ppermute(value, axis, [(i, (i + 1) % count) for i in range(count)])


def neighbours(value, axis):
    return ring(value, axis), lax.ppermute(
        value, axis, [((i + 1) % lax.axis_size(axis), i) for i in range(lax.axis_size(axis))]
    )


def spread(values, masks, stack, row, frame):
    left = pltpu.roll(values, 1, 1) * masks[0]
    right = pltpu.roll(values, W - 1, 1) * masks[1]
    columns = slice(frame * W, (frame + 1) * W)
    for tap, shifted in enumerate((left, values, right)):
        start = row * TAPS + tap * C
        stack[start : start + C, columns] = shifted


def multiply(weights, stack, row, frame):
    total = None
    for tap in range(3):
        window = stack[row * TAPS : (row + 4) * TAPS, (frame + tap) * W : (frame + tap + 2) * W]
        part = jnp.dot(weights[tap], window, preferred_element_type=jnp.float32)
        total = part if total is None else total + part
    return total


def decode_kernel(joined, flags, gain_two, bias_one, bias_two, *rest):
    arrays, rest = rest[:9], rest[9:]
    raw, own, low, high, tail, low_tail, high_tail, weights_one, weights_two = arrays
    boxes, first, second, done, stores = rest[-5:]
    start = SEG if joined else 0

    @pl.when(flags[0] > 0)
    def _():
        lane = lax.broadcasted_iota(jnp.int32, (C, W), 1)
        masks = [
            jnp.where(lane == edge, 0.0, 1.0).astype(jnp.bfloat16) for edge in (0, W - 1)
        ]
        past = flags[1] > 0
        above = flags[2] > 0
        below = flags[3] > 0
        zero = jnp.zeros((), jnp.bfloat16)
        for frames, base, skip, parts in (
            (TAIL, 0, start, (tail, low_tail, high_tail)),
            (SEG, TAIL, 0, (own, low, high)),
        ):
            for frame in range(frames):
                for row in range(2):
                    values = parts[0][frame, row]
                    spread(values, masks, first, 2 + row, base + frame)
                    values = jnp.where(above, parts[1][skip + frame, row], zero)
                    spread(values, masks, first, row, base + frame)
                    values = jnp.where(below, parts[2][skip + frame, row], zero)
                    spread(values, masks, first, 4 + row, base + frame)
        gain = gain_two[...]
        offset = bias_one[...]
        for row in range(0, 4, 2):
            for frame in range(0, SEG + 2, 2):
                total = multiply(weights_one, first, row, frame)
                for k in range(2):
                    for j in range(2):
                        part = total[k * C : (k + 1) * C, j * W : (j + 1) * W] + offset
                        part = part.astype(jnp.bfloat16).astype(jnp.float32)
                        part = activate(part, gain, 0)
                        keep = past if frame < 2 else None
                        side = {0: above, 3: below}.get(row + k)
                        if side is not None:
                            keep = side if keep is None else jnp.logical_and(keep, side)
                        if keep is not None:
                            part = jnp.where(keep, part, 0.0)
                        spread(part.astype(jnp.bfloat16), masks, second, row + k, frame + j)
        offset = bias_two[...]

        def store(block):
            return pltpu.make_async_copy(
                done.at[block], boxes.at[flags[5 + block]], stores.at[block]
            )

        for block in range(RB):
            total = multiply(weights_two, second, 0, block * BF)
            for j in range(BF):
                frame = block * BF + j
                for k in range(2):
                    part = total[k * C : (k + 1) * C, j * W : (j + 1) * W] + offset
                    part = part + raw[frame, k].astype(jnp.float32)
                    part = jnp.where(frame < flags[4], part, 0.0)
                    done[block, j, k] = part.astype(jnp.bfloat16)
            store(block).start()
        for block in range(RB):
            store(block).wait()


def decode(flags, raw, own, sides, tail, tail_sides, weights, vectors, boxes, box_count):
    joined = tail_sides is None
    sides = list(sides) if joined else [*sides, *tail_sides]
    operands = [flags, *vectors, raw, own, *sides[:2], tail, *sides[-2:], *weights]
    specs = [pl.BlockSpec(memory_space=pltpu.SMEM)]
    specs += [pl.BlockSpec(memory_space=pltpu.VMEM)] * (len(operands) - 1)
    aliases = {}
    if boxes is not None:
        aliases = {len(operands): 0}
        operands.append(boxes)
        specs.append(pl.BlockSpec(memory_space=pl.ANY))
    return pl.pallas_call(
        functools.partial(decode_kernel, joined),
        out_shape=jax.ShapeDtypeStruct((box_count, BF, 2, C, W), jnp.bfloat16),
        in_specs=specs,
        out_specs=pl.BlockSpec(memory_space=pl.ANY),
        scratch_shapes=[
            pltpu.VMEM((6 * TAPS, (TAIL + SEG) * W), jnp.bfloat16),
            pltpu.VMEM((4 * TAPS, (2 + SEG) * W), jnp.bfloat16),
            pltpu.VMEM((RB, BF, 2, C, W), jnp.bfloat16),
            pltpu.SemaphoreType.DMA((RB,)),
        ],
        input_output_aliases=aliases,
        compiler_params=pltpu.CompilerParams(vmem_limit_bytes=32 * 2**20),
        cost_estimate=pl.CostEstimate(flops=6 * 10**9, bytes_accessed=4 * 10**6, transcendentals=0),
        name="decode",
    )(*operands)


def pair_kernel(one, two, pair_one, pair_two):
    for weight, pair in ((one, pair_one), (two, pair_two)):
        pair[...] = jnp.zeros(pair.shape, pair.dtype)
        for tap in range(3):
            for row in range(3):
                for cell in range(3):
                    tile = weight[tap, row, cell]
                    for k in range(2):
                        start = ((row + k) * 3 + cell) * C
                        pair[tap, k * C : (k + 1) * C, start : start + C] = tile


def pair_weights(one, two):
    shape = jax.ShapeDtypeStruct((3, 2 * C, 4 * TAPS), jnp.bfloat16)
    return pl.pallas_call(
        pair_kernel,
        out_shape=(shape, shape),
        in_specs=[pl.BlockSpec(memory_space=pltpu.VMEM)] * 2,
        out_specs=[pl.BlockSpec(memory_space=pltpu.VMEM)] * 2,
        compiler_params=pltpu.CompilerParams(vmem_limit_bytes=32 * 2**20),
        name="pair_weights",
    )(one, two)


def local(
    features, frame_counts, places, gain_one, gain_two, conv_one, conv_two, bias_one, bias_two
):
    my_video = lax.axis_index("video")
    my_tm = lax.axis_index("tm")
    my_height = lax.axis_index("height")
    videos = lax.axis_size("video")
    tm_count = lax.axis_size("tm")
    heights = lax.axis_size("height")
    rounds = features.shape[1]

    raw = jnp.swapaxes(features[0], 2, 3)
    own = activate(raw.astype(jnp.float32), gain_one[:, None], 3).astype(jnp.bfloat16)
    leads = my_tm == 0
    past_0, past_1 = (ring(own[turn, SEG - TAIL :], "tm") for turn in range(rounds))
    tail_0 = jnp.where(leads, jnp.zeros((), jnp.bfloat16), past_0)
    tail_1 = jnp.where(leads, past_0, past_1)
    sides_0 = neighbours(own[0], "height")
    tail_sides_0 = neighbours(tail_0, "height")
    sides_1 = neighbours(jnp.concatenate([own[1], tail_1]), "height")

    held = lax.dynamic_index_in_dim(
        places.reshape(videos, rounds, tm_count, RB), my_tm, 2, keepdims=False
    )
    mine = lax.dynamic_index_in_dim(held, my_video, 0, keepdims=False)
    count = lax.dynamic_index_in_dim(frame_counts, my_video, 0, keepdims=False)
    owner = mine // (SLOTS * tm_count)
    flags = []
    for turn in range(rounds):
        live = count > turn * tm_count * SEG
        past = jnp.logical_or(turn > 0, my_tm > 0)
        limit = count - (turn * tm_count + my_tm) * SEG
        head = jnp.stack([live, past, my_height > 0, my_height < heights - 1, limit])
        flags.append(jnp.concatenate([head, jnp.minimum(owner[turn], videos - 1)]).astype(jnp.int32))

    wide = [jnp.broadcast_to(v[:, None], (C, W)) for v in (gain_two, bias_one, bias_two)]
    weights = pair_weights(conv_one, conv_two)
    boxes = decode(
        flags[0], raw[0], own[0], sides_0, tail_0, tail_sides_0, weights, wide, None, videos
    )
    boxes = decode(flags[1], raw[1], own[1], sides_1, tail_1, None, weights, wide, boxes, videos)
    received = lax.all_to_all(boxes, "video", split_axis=0, concat_axis=0, tiled=True)

    wanted = (my_video * tm_count + my_tm) * SLOTS + jnp.arange(SLOTS)
    match = (held.reshape(videos, -1)[None] == wanted[:, None, None]).astype(jnp.int32)
    found = jnp.sum(match, axis=(1, 2)) > 0
    source = jnp.sum(match * jnp.arange(videos)[None, :, None], axis=(1, 2))
    chosen = jnp.take(received, source, axis=0, mode="clip")
    chosen = jnp.where(found[:, None, None, None, None], chosen, jnp.zeros((), jnp.bfloat16))
    return jnp.swapaxes(chosen, 2, 3).reshape(1, SLOTS * BF, C, 2, W)


def solution(mesh):
    placed = (P("video", None, "tm", None, "height", None), P(), P(), P(), P(), P(), P(), P(), P())
    return jax.shard_map(
        local,
        mesh=mesh,
        in_specs=placed,
        out_specs=P("video", "tm", None, "height", None),
        check_vma=False,
    )
```

```python
import functools

import jax
import jax.numpy as jnp
from jax import lax
from jax.experimental import pallas as pl
from jax.experimental.pallas import tpu as pltpu
from jax.sharding import PartitionSpec as P

EPS = 1e-06
BF = 2
RB = 4
SEG = BF * RB
TAIL = 2 * BF
C = 96
W = 128
TAPS = 3 * C
SLOTS = 5


def activate(values, gain, axis):
    mean_square = jnp.mean(values * values, axis=axis, keepdims=True)
    scaled = values * lax.rsqrt(mean_square + EPS) * gain
    return scaled * (0.5 * jnp.tanh(0.5 * scaled) + 0.5)


def ring(value, axis):
    count = lax.axis_size(axis)
    return lax.ppermute(value, axis, [(i, (i + 1) % count) for i in range(count)])


def neighbours(value, axis):
    return ring(value, axis), lax.ppermute(
        value, axis, [((i + 1) % lax.axis_size(axis), i) for i in range(lax.axis_size(axis))]
    )


def spread(values, masks, stack, row, frame):
    left = pltpu.roll(values, 1, 1) * masks[0]
    right = pltpu.roll(values, W - 1, 1) * masks[1]
    columns = slice(frame * W, (frame + 1) * W)
    for tap, shifted in enumerate((left, values, right)):
        start = row * TAPS + tap * C
        stack[start : start + C, columns] = shifted


def multiply(weights, stack, row, frame):
    total = None
    for tap in range(3):
        window = stack[row * TAPS : (row + 4) * TAPS, (frame + tap) * W : (frame + tap + 2) * W]
        part = jnp.dot(weights[tap], window, preferred_element_type=jnp.float32)
        total = part if total is None else total + part
    return total


def decode_kernel(joined, flags, gain_two, bias_one, bias_two, *rest):
    arrays, rest = rest[:9], rest[9:]
    raw, own, low, high, tail, low_tail, high_tail, *sources = arrays
    boxes, first, second, done, weights_one, weights_two, loads, stores = rest[-8:]
    start = SEG if joined else 0

    def load(k):
        return pltpu.make_async_copy(sources[k], (weights_one, weights_two)[k], loads.at[k])

    @pl.when(flags[0] > 0)
    def _():
        load(0).start()
        load(1).start()
        lane = lax.broadcasted_iota(jnp.int32, (C, W), 1)
        masks = [
            jnp.where(lane == edge, 0.0, 1.0).astype(jnp.bfloat16) for edge in (0, W - 1)
        ]
        past = flags[1] > 0
        above = flags[2] > 0
        below = flags[3] > 0
        zero = jnp.zeros((), jnp.bfloat16)
        for frames, base, skip, parts in (
            (TAIL, 0, start, (tail, low_tail, high_tail)),
            (SEG, TAIL, 0, (own, low, high)),
        ):
            for frame in range(frames):
                for row in range(2):
                    values = parts[0][frame, row]
                    spread(values, masks, first, 2 + row, base + frame)
                    values = jnp.where(above, parts[1][skip + frame, row], zero)
                    spread(values, masks, first, row, base + frame)
                    values = jnp.where(below, parts[2][skip + frame, row], zero)
                    spread(values, masks, first, 4 + row, base + frame)
        load(0).wait()
        gain = gain_two[...]
        offset = bias_one[...]
        for row in range(0, 4, 2):
            for frame in range(0, SEG + 2, 2):
                total = multiply(weights_one, first, row, frame)
                for k in range(2):
                    for j in range(2):
                        part = total[k * C : (k + 1) * C, j * W : (j + 1) * W] + offset
                        part = part.astype(jnp.bfloat16).astype(jnp.float32)
                        part = activate(part, gain, 0)
                        keep = past if frame < 2 else None
                        side = {0: above, 3: below}.get(row + k)
                        if side is not None:
                            keep = side if keep is None else jnp.logical_and(keep, side)
                        if keep is not None:
                            part = jnp.where(keep, part, 0.0)
                        spread(part.astype(jnp.bfloat16), masks, second, row + k, frame + j)
        load(1).wait()
        offset = bias_two[...]

        def store(block):
            return pltpu.make_async_copy(
                done.at[block], boxes.at[flags[5 + block]], stores.at[block]
            )

        for block in range(RB):
            total = multiply(weights_two, second, 0, block * BF)
            for j in range(BF):
                frame = block * BF + j
                for k in range(2):
                    part = total[k * C : (k + 1) * C, j * W : (j + 1) * W] + offset
                    part = part + raw[frame, k].astype(jnp.float32)
                    part = jnp.where(frame < flags[4], part, 0.0)
                    done[block, j, k] = part.astype(jnp.bfloat16)
            store(block).start()
        for block in range(RB):
            store(block).wait()


def decode(flags, raw, own, sides, tail, tail_sides, weights, vectors, boxes, box_count):
    joined = tail_sides is None
    sides = list(sides) if joined else [*sides, *tail_sides]
    operands = [flags, *vectors, raw, own, *sides[:2], tail, *sides[-2:], *weights]
    specs = [pl.BlockSpec(memory_space=pltpu.SMEM)]
    specs += [pl.BlockSpec(memory_space=pltpu.VMEM)] * (len(operands) - 3)
    specs += [pl.BlockSpec(memory_space=pl.ANY)] * 2
    aliases = {}
    if boxes is not None:
        aliases = {len(operands): 0}
        operands.append(boxes)
        specs.append(pl.BlockSpec(memory_space=pl.ANY))
    return pl.pallas_call(
        functools.partial(decode_kernel, joined),
        out_shape=jax.ShapeDtypeStruct((box_count, BF, 2, C, W), jnp.bfloat16),
        in_specs=specs,
        out_specs=pl.BlockSpec(memory_space=pl.ANY),
        scratch_shapes=[
            pltpu.VMEM((6 * TAPS, (TAIL + SEG) * W), jnp.bfloat16),
            pltpu.VMEM((4 * TAPS, (2 + SEG) * W), jnp.bfloat16),
            pltpu.VMEM((RB, BF, 2, C, W), jnp.bfloat16),
            *[pltpu.VMEM(weight.shape, jnp.bfloat16) for weight in weights],
            pltpu.SemaphoreType.DMA((2,)),
            pltpu.SemaphoreType.DMA((RB,)),
        ],
        input_output_aliases=aliases,
        compiler_params=pltpu.CompilerParams(vmem_limit_bytes=32 * 2**20),
        cost_estimate=pl.CostEstimate(flops=6 * 10**9, bytes_accessed=4 * 10**6, transcendentals=0),
        name="decode",
    )(*operands)


def pair_kernel(one, two, pair_one, pair_two):
    for weight, pair in ((one, pair_one), (two, pair_two)):
        pair[...] = jnp.zeros(pair.shape, pair.dtype)
        for tap in range(3):
            for row in range(3):
                for cell in range(3):
                    tile = weight[tap, row, cell]
                    for k in range(2):
                        start = ((row + k) * 3 + cell) * C
                        pair[tap, k * C : (k + 1) * C, start : start + C] = tile


def pair_weights(one, two):
    shape = jax.ShapeDtypeStruct((3, 2 * C, 4 * TAPS), jnp.bfloat16)
    return pl.pallas_call(
        pair_kernel,
        out_shape=(shape, shape),
        in_specs=[pl.BlockSpec(memory_space=pltpu.VMEM)] * 2,
        out_specs=[pl.BlockSpec(memory_space=pltpu.VMEM)] * 2,
        compiler_params=pltpu.CompilerParams(vmem_limit_bytes=32 * 2**20),
        name="pair_weights",
    )(one, two)


def local(
    features, frame_counts, places, gain_one, gain_two, conv_one, conv_two, bias_one, bias_two
):
    my_video = lax.axis_index("video")
    my_tm = lax.axis_index("tm")
    my_height = lax.axis_index("height")
    videos = lax.axis_size("video")
    tm_count = lax.axis_size("tm")
    heights = lax.axis_size("height")
    rounds = features.shape[1]

    raw, own = [], []
    for turn in range(rounds):
        raw.append(jnp.swapaxes(features[0, turn], 1, 2))
        values = raw[turn].astype(jnp.float32)
        own.append(activate(values, gain_one[:, None], 2).astype(jnp.bfloat16))
    past_0, past_1 = (ring(value[SEG - TAIL :], "tm") for value in own)
    sides_0 = neighbours(own[0], "height")

    held = lax.dynamic_index_in_dim(
        places.reshape(videos, rounds, tm_count, RB), my_tm, 2, keepdims=False
    )
    mine = lax.dynamic_index_in_dim(held, my_video, 0, keepdims=False)
    count = lax.dynamic_index_in_dim(frame_counts, my_video, 0, keepdims=False)
    owner = mine // (SLOTS * tm_count)
    flags = []
    for turn in range(rounds):
        live = count > turn * tm_count * SEG
        past = jnp.logical_or(turn > 0, my_tm > 0)
        limit = count - (turn * tm_count + my_tm) * SEG
        head = jnp.stack([live, past, my_height > 0, my_height < heights - 1, limit])
        flags.append(jnp.concatenate([head, jnp.minimum(owner[turn], videos - 1)]).astype(jnp.int32))

    wide = [jnp.broadcast_to(v[:, None], (C, W)) for v in (gain_two, bias_one, bias_two)]
    weights = pair_weights(conv_one, conv_two)
    wanted = (my_video * tm_count + my_tm) * SLOTS + jnp.arange(SLOTS)
    match = (held.reshape(videos, -1)[None] == wanted[:, None, None]).astype(jnp.int32)
    found = jnp.sum(match, axis=(1, 2)) > 0
    source = jnp.sum(match * jnp.arange(videos)[None, :, None], axis=(1, 2))

    past_0, past_1, flags, wide, weights, found, source = lax.optimization_barrier(
        (past_0, past_1, flags, wide, weights, found, source)
    )
    leads = my_tm == 0
    tail_0 = jnp.where(leads, jnp.zeros((), jnp.bfloat16), past_0)
    tail_1 = jnp.where(leads, past_0, past_1)
    tail_sides_0 = neighbours(tail_0, "height")
    sides_0, joined = lax.optimization_barrier((sides_0, jnp.concatenate([own[1], tail_1])))
    sides_1 = neighbours(joined, "height")
    boxes = decode(
        flags[0], raw[0], own[0], sides_0, tail_0, tail_sides_0, weights, wide, None, videos
    )
    boxes = decode(flags[1], raw[1], own[1], sides_1, tail_1, None, weights, wide, boxes, videos)
    received = lax.all_to_all(boxes, "video", split_axis=0, concat_axis=0, tiled=True)
    chosen = jnp.take(received, source, axis=0, mode="clip")
    chosen = jnp.where(found[:, None, None, None, None], chosen, jnp.zeros((), jnp.bfloat16))
    return jnp.swapaxes(chosen, 2, 3).reshape(1, SLOTS * BF, C, 2, W)


def solution(mesh):
    placed = (P("video", None, "tm", None, "height", None), P(), P(), P(), P(), P(), P(), P(), P())
    return jax.shard_map(
        local,
        mesh=mesh,
        in_specs=placed,
        out_specs=P("video", "tm", None, "height", None),
        check_vma=False,
    )
```

```python
import functools

import jax
import jax.numpy as jnp
from jax import lax
from jax.experimental import pallas as pl
from jax.experimental.pallas import tpu as pltpu
from jax.sharding import PartitionSpec as P

EPS = 1e-06
BF = 2
RB = 4
SEG = BF * RB
TAIL = 2 * BF
C = 96
W = 128
TAPS = 3 * C
SLOTS = 5


def activate(values, gain, axis):
    mean_square = jnp.mean(values * values, axis=axis, keepdims=True)
    scaled = values * lax.rsqrt(mean_square + EPS) * gain
    return scaled * (0.5 * jnp.tanh(0.5 * scaled) + 0.5)


def ring(value, axis):
    count = lax.axis_size(axis)
    return lax.ppermute(value, axis, [(i, (i + 1) % count) for i in range(count)])


def neighbours(value, axis):
    return ring(value, axis), lax.ppermute(
        value, axis, [((i + 1) % lax.axis_size(axis), i) for i in range(lax.axis_size(axis))]
    )


def spread(values, masks, stack, row, frame):
    left = pltpu.roll(values, 1, 1) * masks[0]
    right = pltpu.roll(values, W - 1, 1) * masks[1]
    columns = slice(frame * W, (frame + 1) * W)
    for tap, shifted in enumerate((left, values, right)):
        start = row * TAPS + tap * C
        stack[start : start + C, columns] = shifted


def multiply(weights, stack, row, frame):
    total = None
    for tap in range(3):
        window = stack[row * TAPS : (row + 4) * TAPS, (frame + tap) * W : (frame + tap + 2) * W]
        part = jnp.dot(weights[tap], window, preferred_element_type=jnp.float32)
        total = part if total is None else total + part
    return total


def decode_kernel(joined, flags, gain_two, bias_one, bias_two, *rest):
    arrays, rest = rest[:9], rest[9:]
    raw, own, low, high, tail, low_tail, high_tail, *plain = arrays
    boxes, first, second, done, weights_one, weights_two, stores = rest[-7:]
    skip = SEG if joined else 0

    @pl.when(flags[0] > 0)
    def _():
        lane = lax.broadcasted_iota(jnp.int32, (C, W), 1)
        masks = [
            jnp.where(lane == edge, 0.0, 1.0).astype(jnp.bfloat16) for edge in (0, W - 1)
        ]
        past = flags[1] > 0
        above = flags[2] > 0
        below = flags[3] > 0
        zero = jnp.zeros((), jnp.bfloat16)
        pair_weights(plain[0], weights_one)
        for frames, base, start, parts in (
            (TAIL, 0, skip, (tail, low_tail, high_tail)),
            (SEG, TAIL, 0, (own, low, high)),
        ):
            for frame in range(frames):
                for row in range(2):
                    values = parts[0][frame, row]
                    spread(values, masks, first, 2 + row, base + frame)
                    values = jnp.where(above, parts[1][start + frame, row], zero)
                    spread(values, masks, first, row, base + frame)
                    values = jnp.where(below, parts[2][start + frame, row], zero)
                    spread(values, masks, first, 4 + row, base + frame)
        gain = gain_two[...]
        offset = bias_one[...]
        for row in range(0, 4, 2):
            for frame in range(0, SEG + 2, 2):
                total = multiply(weights_one, first, row, frame)
                for k in range(2):
                    for j in range(2):
                        part = total[k * C : (k + 1) * C, j * W : (j + 1) * W] + offset
                        part = part.astype(jnp.bfloat16).astype(jnp.float32)
                        part = activate(part, gain, 0)
                        keep = past if frame < 2 else None
                        side = {0: above, 3: below}.get(row + k)
                        if side is not None:
                            keep = side if keep is None else jnp.logical_and(keep, side)
                        if keep is not None:
                            part = jnp.where(keep, part, 0.0)
                        spread(part.astype(jnp.bfloat16), masks, second, row + k, frame + j)
        pair_weights(plain[1], weights_two)
        offset = bias_two[...]

        def store(block):
            return pltpu.make_async_copy(
                done.at[block], boxes.at[flags[5 + block]], stores.at[block]
            )

        for block in range(RB):
            total = multiply(weights_two, second, 0, block * BF)
            for j in range(BF):
                frame = block * BF + j
                for k in range(2):
                    part = total[k * C : (k + 1) * C, j * W : (j + 1) * W] + offset
                    part = part + raw[frame, k].astype(jnp.float32)
                    part = jnp.where(frame < flags[4], part, 0.0)
                    done[block, j, k] = part.astype(jnp.bfloat16)
            store(block).start()
        for block in range(RB):
            store(block).wait()


def decode(flags, raw, own, sides, tail, tail_sides, weights, vectors, boxes, box_count):
    joined = tail_sides is None
    sides = list(sides) if joined else [*sides, *tail_sides]
    operands = [flags, *vectors, raw, own, *sides[:2], tail, *sides[-2:], *weights]
    specs = [pl.BlockSpec(memory_space=pltpu.SMEM)]
    specs += [pl.BlockSpec(memory_space=pltpu.VMEM)] * (len(operands) - 1)
    aliases = {}
    if boxes is not None:
        aliases = {len(operands): 0}
        operands.append(boxes)
        specs.append(pl.BlockSpec(memory_space=pl.ANY))
    paired = pltpu.VMEM((3, 2 * C, 4 * TAPS), jnp.bfloat16)
    return pl.pallas_call(
        functools.partial(decode_kernel, joined),
        out_shape=jax.ShapeDtypeStruct((box_count, BF, 2, C, W), jnp.bfloat16),
        in_specs=specs,
        out_specs=pl.BlockSpec(memory_space=pl.ANY),
        scratch_shapes=[
            pltpu.VMEM((6 * TAPS, (TAIL + SEG) * W), jnp.bfloat16),
            pltpu.VMEM((4 * TAPS, (2 + SEG) * W), jnp.bfloat16),
            pltpu.VMEM((RB, BF, 2, C, W), jnp.bfloat16),
            paired,
            paired,
            pltpu.SemaphoreType.DMA((RB,)),
        ],
        input_output_aliases=aliases,
        compiler_params=pltpu.CompilerParams(vmem_limit_bytes=32 * 2**20),
        cost_estimate=pl.CostEstimate(flops=6 * 10**9, bytes_accessed=4 * 10**6, transcendentals=0),
        name="decode",
    )(*operands)


def pair_weights(weight, pair):
    pair[:, :C, 3 * TAPS :] = jnp.zeros((3, C, TAPS), jnp.bfloat16)
    pair[:, C:, :TAPS] = jnp.zeros((3, C, TAPS), jnp.bfloat16)
    for tap in range(3):
        for row in range(3):
            for cell in range(3):
                tile = weight[tap, row, cell]
                for k in range(2):
                    start = ((row + k) * 3 + cell) * C
                    pair[tap, k * C : (k + 1) * C, start : start + C] = tile


def local(
    features, frame_counts, places, gain_one, gain_two, conv_one, conv_two, bias_one, bias_two
):
    my_video = lax.axis_index("video")
    my_tm = lax.axis_index("tm")
    my_height = lax.axis_index("height")
    videos = lax.axis_size("video")
    tm_count = lax.axis_size("tm")
    heights = lax.axis_size("height")
    rounds = features.shape[1]

    raw, own = [], []
    for turn in range(rounds):
        raw.append(jnp.swapaxes(features[0, turn], 1, 2))
        values = raw[turn].astype(jnp.float32)
        own.append(activate(values, gain_one[:, None], 2).astype(jnp.bfloat16))
    past_0, past_1 = (ring(value[SEG - TAIL :], "tm") for value in own)
    sides_0 = neighbours(own[0], "height")

    held = lax.dynamic_index_in_dim(
        places.reshape(videos, rounds, tm_count, RB), my_tm, 2, keepdims=False
    )
    mine = lax.dynamic_index_in_dim(held, my_video, 0, keepdims=False)
    count = lax.dynamic_index_in_dim(frame_counts, my_video, 0, keepdims=False)
    owner = mine // (SLOTS * tm_count)
    flags = []
    for turn in range(rounds):
        live = count > turn * tm_count * SEG
        past = jnp.logical_or(turn > 0, my_tm > 0)
        limit = count - (turn * tm_count + my_tm) * SEG
        head = jnp.stack([live, past, my_height > 0, my_height < heights - 1, limit])
        flags.append(jnp.concatenate([head, jnp.minimum(owner[turn], videos - 1)]).astype(jnp.int32))

    wide = [jnp.broadcast_to(v[:, None], (C, W)) for v in (gain_two, bias_one, bias_two)]
    weights = (conv_one, conv_two)
    wanted = (my_video * tm_count + my_tm) * SLOTS + jnp.arange(SLOTS)
    match = (held.reshape(videos, -1)[None] == wanted[:, None, None]).astype(jnp.int32)
    found = jnp.sum(match, axis=(1, 2)) > 0
    source = jnp.sum(match * jnp.arange(videos)[None, :, None], axis=(1, 2))

    past_0, past_1, flags, wide, found, source = lax.optimization_barrier(
        (past_0, past_1, flags, wide, found, source)
    )
    leads = my_tm == 0
    tail_0 = jnp.where(leads, jnp.zeros((), jnp.bfloat16), past_0)
    tail_1 = jnp.where(leads, past_0, past_1)
    tail_sides_0 = neighbours(tail_0, "height")
    ends = [side[-1, -1, -1, -1:] for side in sides_0]
    joined, _ = lax.optimization_barrier((jnp.concatenate([own[1], tail_1]), ends))
    sides_1 = neighbours(joined, "height")
    boxes = decode(
        flags[0], raw[0], own[0], sides_0, tail_0, tail_sides_0, weights, wide, None, videos
    )
    boxes = decode(flags[1], raw[1], own[1], sides_1, tail_1, None, weights, wide, boxes, videos)
    received = lax.all_to_all(boxes, "video", split_axis=0, concat_axis=0, tiled=True)
    chosen = jnp.take(received, source, axis=0, mode="clip")
    chosen = jnp.where(found[:, None, None, None, None], chosen, jnp.zeros((), jnp.bfloat16))
    return jnp.swapaxes(chosen, 2, 3).reshape(1, SLOTS * BF, C, 2, W)


def solution(mesh):
    placed = (P("video", None, "tm", None, "height", None), P(), P(), P(), P(), P(), P(), P(), P())
    return jax.shard_map(
        local,
        mesh=mesh,
        in_specs=placed,
        out_specs=P("video", "tm", None, "height", None),
        check_vma=False,
    )
```

```python
import functools
import itertools

import jax
import jax.numpy as jnp
from jax import lax
from jax.experimental import pallas as pl
from jax.experimental.pallas import tpu as pltpu
from jax.sharding import PartitionSpec as P

EPS = 1e-06
BF = 2
RB = 4
SEG = BF * RB
TAIL = 2 * BF
C = 96
W = 128
TAPS = 3 * C
SLOTS = 5


def activate(values, gain, axis):
    mean_square = jnp.mean(values * values, axis=axis, keepdims=True)
    scaled = values * lax.rsqrt(mean_square + EPS) * gain
    return scaled * (0.5 * jnp.tanh(0.5 * scaled) + 0.5)


def shifted(value, *steps):
    axes = tuple(axis for axis, _ in steps)
    sizes = [lax.axis_size(axis) for axis in axes]
    pairs = []
    for source in itertools.product(*map(range, sizes)):
        target = [(at + step) % size for at, (_, step), size in zip(source, steps, sizes)]
        index = [0, 0]
        for at, to, size in zip(source, target, sizes):
            index = [index[0] * size + at, index[1] * size + to]
        pairs.append(tuple(index))
    return lax.ppermute(value, axes, pairs)


def spread(values, masks, stack, row, frame):
    left = pltpu.roll(values, 1, 1) * masks[0]
    right = pltpu.roll(values, W - 1, 1) * masks[1]
    columns = slice(frame * W, (frame + 1) * W)
    for tap, shifted in enumerate((left, values, right)):
        start = row * TAPS + tap * C
        stack[start : start + C, columns] = shifted


def multiply(weights, stack, row, frame):
    total = None
    for tap in range(3):
        window = stack[row * TAPS : (row + 4) * TAPS, (frame + tap) * W : (frame + tap + 2) * W]
        part = jnp.dot(weights[tap], window, preferred_element_type=jnp.float32)
        total = part if total is None else total + part
    return total


def decode_kernel(turn, flags, gain_two, bias_one, bias_two, *rest):
    plain, raw, own, low, high = rest[:2], *rest[2:6]
    tails, earlier_tails = rest[6:9], rest[9:12]
    boxes, first, second, done, weights_one, weights_two, stores = rest[-7:]

    @pl.when(flags[0] > 0)
    def _():
        lane = lax.broadcasted_iota(jnp.int32, (C, W), 1)
        masks = [
            jnp.where(lane == edge, 0.0, 1.0).astype(jnp.bfloat16) for edge in (0, W - 1)
        ]
        leads = flags[1] > 0
        above = flags[2] > 0
        below = flags[3] > 0
        zero = jnp.zeros((), jnp.bfloat16)
        pair_weights(plain[0], weights_one)
        for frame in range(TAIL):
            for row in range(6):
                values = tails[row // 2][frame, row % 2]
                other = earlier_tails[row // 2][frame, row % 2] if turn > 0 else zero
                values = jnp.where(leads, other, values)
                if row // 2 != 1:
                    values = jnp.where(above if row < 2 else below, values, zero)
                spread(values, masks, first, row, frame)
        for frame in range(SEG):
            for row in range(6):
                values = (low, own, high)[row // 2][frame, row % 2]
                if row // 2 != 1:
                    values = jnp.where(above if row < 2 else below, values, zero)
                spread(values, masks, first, row, TAIL + frame)
        gain = gain_two[...]
        offset = bias_one[...]
        for row in range(0, 4, 2):
            for frame in range(0, SEG + 2, 2):
                total = multiply(weights_one, first, row, frame)
                for k in range(2):
                    for j in range(2):
                        part = total[k * C : (k + 1) * C, j * W : (j + 1) * W] + offset
                        part = part.astype(jnp.bfloat16).astype(jnp.float32)
                        part = activate(part, gain, 0)
                        keep = jnp.logical_not(leads) if turn == 0 and frame < 2 else None
                        side = {0: above, 3: below}.get(row + k)
                        if side is not None:
                            keep = side if keep is None else jnp.logical_and(keep, side)
                        if keep is not None:
                            part = jnp.where(keep, part, 0.0)
                        spread(part.astype(jnp.bfloat16), masks, second, row + k, frame + j)
        pair_weights(plain[1], weights_two)
        offset = bias_two[...]

        def store(block):
            return pltpu.make_async_copy(
                done.at[block], boxes.at[flags[5 + block]], stores.at[block]
            )

        for block in range(RB):
            total = multiply(weights_two, second, 0, block * BF)
            for j in range(BF):
                frame = block * BF + j
                for k in range(2):
                    part = total[k * C : (k + 1) * C, j * W : (j + 1) * W] + offset
                    part = part + raw[frame, k].astype(jnp.float32)
                    part = jnp.where(frame < flags[4], part, 0.0)
                    done[block, j, k] = part.astype(jnp.bfloat16)
            store(block).start()
        for block in range(RB):
            store(block).wait()


def decode(turn, flags, vectors, weights, raw, own, sides, tails, boxes, box_count):
    operands = [flags, *vectors, *weights, raw, own, *sides, *tails]
    specs = [pl.BlockSpec(memory_space=pltpu.SMEM)]
    specs += [pl.BlockSpec(memory_space=pltpu.VMEM)] * (len(operands) - 1)
    aliases = {}
    if boxes is not None:
        aliases = {len(operands): 0}
        operands.append(boxes)
        specs.append(pl.BlockSpec(memory_space=pl.ANY))
    paired = pltpu.VMEM((3, 2 * C, 4 * TAPS), jnp.bfloat16)
    return pl.pallas_call(
        functools.partial(decode_kernel, turn),
        out_shape=jax.ShapeDtypeStruct((box_count, BF, 2, C, W), jnp.bfloat16),
        in_specs=specs,
        out_specs=pl.BlockSpec(memory_space=pl.ANY),
        scratch_shapes=[
            pltpu.VMEM((6 * TAPS, (TAIL + SEG) * W), jnp.bfloat16),
            pltpu.VMEM((4 * TAPS, (2 + SEG) * W), jnp.bfloat16),
            pltpu.VMEM((RB, BF, 2, C, W), jnp.bfloat16),
            paired,
            paired,
            pltpu.SemaphoreType.DMA((RB,)),
        ],
        input_output_aliases=aliases,
        compiler_params=pltpu.CompilerParams(vmem_limit_bytes=32 * 2**20),
        cost_estimate=pl.CostEstimate(flops=6 * 10**9, bytes_accessed=4 * 10**6, transcendentals=0),
        name="decode",
    )(*operands)


def pair_weights(weight, pair):
    pair[:, :C, 3 * TAPS :] = jnp.zeros((3, C, TAPS), jnp.bfloat16)
    pair[:, C:, :TAPS] = jnp.zeros((3, C, TAPS), jnp.bfloat16)
    for tap in range(3):
        for row in range(3):
            for cell in range(3):
                tile = weight[tap, row, cell]
                for k in range(2):
                    start = ((row + k) * 3 + cell) * C
                    pair[tap, k * C : (k + 1) * C, start : start + C] = tile


def local(
    features, frame_counts, places, gain_one, gain_two, conv_one, conv_two, bias_one, bias_two
):
    my_video = lax.axis_index("video")
    my_tm = lax.axis_index("tm")
    my_height = lax.axis_index("height")
    videos = lax.axis_size("video")
    tm_count = lax.axis_size("tm")
    heights = lax.axis_size("height")
    rounds = features.shape[1]

    raw, own = [], []
    for turn in range(rounds):
        raw.append(jnp.swapaxes(features[0, turn], 1, 2))
        values = raw[turn].astype(jnp.float32)
        own.append(activate(values, gain_one[:, None], 2).astype(jnp.bfloat16))
    sides, tails = [], []
    for value in own:
        end = value[SEG - TAIL :]
        sides.append([shifted(value, ("height", 1)), shifted(value, ("height", -1))])
        tails.append(
            [
                shifted(end, ("tm", 1), ("height", 1)),
                shifted(end, ("tm", 1)),
                shifted(end, ("tm", 1), ("height", -1)),
            ]
        )

    held = lax.dynamic_index_in_dim(
        places.reshape(videos, rounds, tm_count, RB), my_tm, 2, keepdims=False
    )
    mine = lax.dynamic_index_in_dim(held, my_video, 0, keepdims=False)
    count = lax.dynamic_index_in_dim(frame_counts, my_video, 0, keepdims=False)
    owner = mine // (SLOTS * tm_count)
    flags = []
    for turn in range(rounds):
        live = count > turn * tm_count * SEG
        limit = count - (turn * tm_count + my_tm) * SEG
        head = jnp.stack([live, my_tm == 0, my_height > 0, my_height < heights - 1, limit])
        flags.append(jnp.concatenate([head, jnp.minimum(owner[turn], videos - 1)]).astype(jnp.int32))

    wide = [jnp.broadcast_to(v[:, None], (C, W)) for v in (gain_two, bias_one, bias_two)]
    weights = (conv_one, conv_two)
    wanted = (my_video * tm_count + my_tm) * SLOTS + jnp.arange(SLOTS)
    match = (held.reshape(videos, -1)[None] == wanted[:, None, None]).astype(jnp.int32)
    found = jnp.sum(match, axis=(1, 2)) > 0
    source = jnp.sum(match * jnp.arange(videos)[None, :, None], axis=(1, 2))

    boxes = None
    for turn in range(rounds):
        known = tails[turn] + tails[turn - 1] if turn > 0 else tails[turn]
        boxes = decode(
            turn, flags[turn], wide, weights, raw[turn], own[turn], sides[turn], known, boxes, videos
        )
    received = lax.all_to_all(boxes, "video", split_axis=0, concat_axis=0, tiled=True)
    chosen = jnp.take(received, source, axis=0, mode="clip")
    chosen = jnp.where(found[:, None, None, None, None], chosen, jnp.zeros((), jnp.bfloat16))
    return jnp.swapaxes(chosen, 2, 3).reshape(1, SLOTS * BF, C, 2, W)


def solution(mesh):
    placed = (P("video", None, "tm", None, "height", None), P(), P(), P(), P(), P(), P(), P(), P())
    return jax.shard_map(
        local,
        mesh=mesh,
        in_specs=placed,
        out_specs=P("video", "tm", None, "height", None),
        check_vma=False,
    )
```

```python
import functools

import jax
import jax.numpy as jnp
from jax import lax
from jax.experimental import pallas as pl
from jax.experimental.pallas import tpu as pltpu
from jax.sharding import PartitionSpec as P

EPS = 1e-06
BF = 2
RB = 4
SEG = BF * RB
HALF = SEG // 2
TAIL = 2 * BF
C = 96
W = 128
TAPS = 3 * C
SLOTS = 5


def activate(values, gain, axis):
    mean_square = jnp.mean(values * values, axis=axis, keepdims=True)
    scaled = values * lax.rsqrt(mean_square + EPS) * gain
    return scaled * (0.5 * jnp.tanh(0.5 * scaled) + 0.5)


def ring(value, axis, step):
    count = lax.axis_size(axis)
    return lax.ppermute(value, axis, [(i, (i + step) % count) for i in range(count)])


def spread(values, masks, stack, row, frame):
    left = pltpu.roll(values, 1, 1) * masks[0]
    right = pltpu.roll(values, W - 1, 1) * masks[1]
    columns = slice(frame * W, (frame + 1) * W)
    for tap, shifted in enumerate((left, values, right)):
        start = row * TAPS + tap * C
        stack[start : start + C, columns] = shifted


def multiply(weights, stack, row, frame):
    total = None
    for tap in range(3):
        window = stack[row * TAPS : (row + 4) * TAPS, (frame + tap) * W : (frame + tap + 2) * W]
        part = jnp.dot(weights[tap], window, preferred_element_type=jnp.float32)
        total = part if total is None else total + part
    return total


def decode_kernel(turn, half, flags, gain_two, bias_one, bias_two, *rest):
    plain, raw, own, low, high, tails = rest[:2], *rest[2:6], rest[6:9]
    boxes, first, second, done, weights_one, weights_two, stores = rest[-7:]

    @pl.when(flags[0] > 0)
    def _():
        lane = lax.broadcasted_iota(jnp.int32, (C, W), 1)
        masks = [
            jnp.where(lane == edge, 0.0, 1.0).astype(jnp.bfloat16) for edge in (0, W - 1)
        ]
        leads = flags[1] > 0
        above = flags[2] > 0
        below = flags[3] > 0
        zero = jnp.zeros((), jnp.bfloat16)
        pair_weights(plain[0], weights_one)
        for frame in range(2 * TAIL):
            for row in range(6):
                part, at = row // 2, row % 2
                place = frame + half * HALF - TAIL
                if place < 0:
                    values = tails[part][turn, frame, at]
                    other = tails[part][turn - 1, frame, at] if turn > 0 else zero
                    values = jnp.where(leads, other, values)
                else:
                    values = (low, own, high)[part][place, at]
                if part != 1:
                    values = jnp.where(above if part == 0 else below, values, zero)
                spread(values, masks, first, row, frame)
        gain = gain_two[...]
        offset = bias_one[...]
        for row in range(0, 4, 2):
            for frame in range(0, HALF + 2, 2):
                total = multiply(weights_one, first, row, frame)
                for k in range(2):
                    for j in range(2):
                        part = total[k * C : (k + 1) * C, j * W : (j + 1) * W] + offset
                        part = part.astype(jnp.bfloat16).astype(jnp.float32)
                        part = activate(part, gain, 0)
                        keep = jnp.logical_not(leads) if turn + half + frame == 0 else None
                        side = {0: above, 3: below}.get(row + k)
                        if side is not None:
                            keep = side if keep is None else jnp.logical_and(keep, side)
                        if keep is not None:
                            part = jnp.where(keep, part, 0.0)
                        spread(part.astype(jnp.bfloat16), masks, second, row + k, frame + j)
        pair_weights(plain[1], weights_two)
        offset = bias_two[...]

        def store(block):
            target = flags[5 + half * HALF // BF + block]
            return pltpu.make_async_copy(done.at[block], boxes.at[target], stores.at[block])

        for block in range(HALF // BF):
            total = multiply(weights_two, second, 0, block * BF)
            for j in range(BF):
                frame = half * HALF + block * BF + j
                for k in range(2):
                    part = total[k * C : (k + 1) * C, j * W : (j + 1) * W] + offset
                    part = part + raw[frame, k].astype(jnp.float32)
                    part = jnp.where(frame < flags[4], part, 0.0)
                    done[block, j, k] = part.astype(jnp.bfloat16)
            store(block).start()
        for block in range(HALF // BF):
            store(block).wait()


def decode(turn, half, flags, vectors, weights, raw, own, sides, tails, boxes, box_count):
    operands = [flags, *vectors, *weights, raw, own, *sides, *tails]
    specs = [pl.BlockSpec(memory_space=pltpu.SMEM)]
    specs += [pl.BlockSpec(memory_space=pltpu.VMEM)] * (len(operands) - 1)
    aliases = {}
    if boxes is not None:
        aliases = {len(operands): 0}
        operands.append(boxes)
        specs.append(pl.BlockSpec(memory_space=pl.ANY))
    paired = pltpu.VMEM((3, 2 * C, 4 * TAPS), jnp.bfloat16)
    return pl.pallas_call(
        functools.partial(decode_kernel, turn, half),
        out_shape=jax.ShapeDtypeStruct((box_count, BF, 2, C, W), jnp.bfloat16),
        in_specs=specs,
        out_specs=pl.BlockSpec(memory_space=pl.ANY),
        scratch_shapes=[
            pltpu.VMEM((6 * TAPS, (TAIL + HALF) * W), jnp.bfloat16),
            pltpu.VMEM((4 * TAPS, (2 + HALF) * W), jnp.bfloat16),
            pltpu.VMEM((HALF // BF, BF, 2, C, W), jnp.bfloat16),
            paired,
            paired,
            pltpu.SemaphoreType.DMA((HALF // BF,)),
        ],
        input_output_aliases=aliases,
        compiler_params=pltpu.CompilerParams(vmem_limit_bytes=32 * 2**20),
        cost_estimate=pl.CostEstimate(flops=4 * 10**9, bytes_accessed=3 * 10**6, transcendentals=0),
        name="decode",
    )(*operands)


def pair_weights(weight, pair):
    pair[:, :C, 3 * TAPS :] = jnp.zeros((3, C, TAPS), jnp.bfloat16)
    pair[:, C:, :TAPS] = jnp.zeros((3, C, TAPS), jnp.bfloat16)
    for tap in range(3):
        for row in range(3):
            for cell in range(3):
                tile = weight[tap, row, cell]
                for k in range(2):
                    start = ((row + k) * 3 + cell) * C
                    pair[tap, k * C : (k + 1) * C, start : start + C] = tile


def local(
    features, frame_counts, places, gain_one, gain_two, conv_one, conv_two, bias_one, bias_two
):
    my_video = lax.axis_index("video")
    my_tm = lax.axis_index("tm")
    my_height = lax.axis_index("height")
    videos = lax.axis_size("video")
    tm_count = lax.axis_size("tm")
    heights = lax.axis_size("height")
    rounds = features.shape[1]

    raw, own = [], []
    for turn in range(rounds):
        raw.append(jnp.swapaxes(features[0, turn], 1, 2))
        values = raw[turn].astype(jnp.float32)
        own.append(activate(values, gain_one[:, None], 2).astype(jnp.bfloat16))
    ends = ring(jnp.stack([value[SEG - TAIL :] for value in own]), "tm", 1)
    sides = [[ring(value, "height", step) for step in (1, -1)] for value in own]
    tails = [ring(ends, "height", 1), ends, ring(ends, "height", -1)]

    held = lax.dynamic_index_in_dim(
        places.reshape(videos, rounds, tm_count, RB), my_tm, 2, keepdims=False
    )
    mine = lax.dynamic_index_in_dim(held, my_video, 0, keepdims=False)
    count = lax.dynamic_index_in_dim(frame_counts, my_video, 0, keepdims=False)
    owner = mine // (SLOTS * tm_count)
    flags = []
    for turn in range(rounds):
        live = count > turn * tm_count * SEG
        limit = count - (turn * tm_count + my_tm) * SEG
        head = jnp.stack([live, my_tm == 0, my_height > 0, my_height < heights - 1, limit])
        flags.append(jnp.concatenate([head, jnp.minimum(owner[turn], videos - 1)]).astype(jnp.int32))

    wide = [jnp.broadcast_to(v[:, None], (C, W)) for v in (gain_two, bias_one, bias_two)]
    weights = (conv_one, conv_two)
    wanted = (my_video * tm_count + my_tm) * SLOTS + jnp.arange(SLOTS)
    match = (held.reshape(videos, -1)[None] == wanted[:, None, None]).astype(jnp.int32)
    found = jnp.sum(match, axis=(1, 2)) > 0
    source = jnp.sum(match * jnp.arange(videos)[None, :, None], axis=(1, 2))

    boxes = None
    for half, turn in ((1, 0), (1, 1), (0, 0), (0, 1)):
        known = tails if half == 0 else []
        boxes = decode(
            turn, half, flags[turn], wide, weights, raw[turn], own[turn], sides[turn], known, boxes, videos
        )
    received = lax.all_to_all(boxes, "video", split_axis=0, concat_axis=0, tiled=True)
    chosen = jnp.take(received, source, axis=0, mode="clip")
    chosen = jnp.where(found[:, None, None, None, None], chosen, jnp.zeros((), jnp.bfloat16))
    return jnp.swapaxes(chosen, 2, 3).reshape(1, SLOTS * BF, C, 2, W)


def solution(mesh):
    placed = (P("video", None, "tm", None, "height", None), P(), P(), P(), P(), P(), P(), P(), P())
    return jax.shard_map(
        local,
        mesh=mesh,
        in_specs=placed,
        out_specs=P("video", "tm", None, "height", None),
        check_vma=False,
    )
```

```python
import functools

import jax
import jax.numpy as jnp
from jax import lax
from jax.experimental import pallas as pl
from jax.experimental.pallas import tpu as pltpu
from jax.sharding import PartitionSpec as P

EPS = 1e-06
BF = 2
RB = 4
SEG = BF * RB
TAIL = 2 * BF
C = 96
W = 128
TAPS = 3 * C
SLOTS = 5


def activate(values, gain, axis):
    mean_square = jnp.mean(values * values, axis=axis, keepdims=True)
    scaled = values * lax.rsqrt(mean_square + EPS) * gain
    return scaled * (0.5 * jnp.tanh(0.5 * scaled) + 0.5)


def ring(value, axis):
    count = lax.axis_size(axis)
    return lax.ppermute(value, axis, [(i, (i + 1) % count) for i in range(count)])


def neighbours(value, axis):
    return ring(value, axis), lax.ppermute(
        value, axis, [((i + 1) % lax.axis_size(axis), i) for i in range(lax.axis_size(axis))]
    )


def spread(values, masks, stack, row, frame):
    left = pltpu.roll(values, 1, 1) * masks[0]
    right = pltpu.roll(values, W - 1, 1) * masks[1]
    columns = slice(frame * W, (frame + 1) * W)
    for tap, shifted in enumerate((left, values, right)):
        start = row * TAPS + tap * C
        stack[start : start + C, columns] = shifted


def multiply(weights, stack, row, frame):
    total = None
    for tap in range(3):
        window = stack[row * TAPS : (row + 4) * TAPS, (frame + tap) * W : (frame + tap + 2) * W]
        part = jnp.dot(weights[tap], window, preferred_element_type=jnp.float32)
        total = part if total is None else total + part
    return total


def decode_kernel(joined, flags, gain_two, bias_one, bias_two, *rest):
    arrays, rest = rest[:9], rest[9:]
    raw, own, low, high, tail, low_tail, high_tail, *plain = arrays
    boxes, first, second, done, weights_one, weights_two, stores = rest[-7:]
    skip = SEG if joined else 0

    @pl.when(flags[0] > 0)
    def _():
        lane = lax.broadcasted_iota(jnp.int32, (C, W), 1)
        masks = [
            jnp.where(lane == edge, 0.0, 1.0).astype(jnp.bfloat16) for edge in (0, W - 1)
        ]
        past = flags[1] > 0
        above = flags[2] > 0
        below = flags[3] > 0
        zero = jnp.zeros((), jnp.bfloat16)
        pair_weights(plain[0], weights_one)
        for frames, base, start, parts in (
            (TAIL, 0, skip, (tail, low_tail, high_tail)),
            (SEG, TAIL, 0, (own, low, high)),
        ):
            known = True if joined or base > 0 else past
            for frame in range(frames):
                for row in range(2):
                    values = jnp.where(known, parts[0][frame, row], zero)
                    spread(values, masks, first, 2 + row, base + frame)
                    keep = jnp.logical_and(known, above)
                    values = jnp.where(keep, parts[1][start + frame, row], zero)
                    spread(values, masks, first, row, base + frame)
                    keep = jnp.logical_and(known, below)
                    values = jnp.where(keep, parts[2][start + frame, row], zero)
                    spread(values, masks, first, 4 + row, base + frame)
        gain = gain_two[...]
        offset = bias_one[...]
        for row in range(0, 4, 2):
            for frame in range(0, SEG + 2, 2):
                total = multiply(weights_one, first, row, frame)
                for k in range(2):
                    for j in range(2):
                        part = total[k * C : (k + 1) * C, j * W : (j + 1) * W] + offset
                        part = part.astype(jnp.bfloat16).astype(jnp.float32)
                        part = activate(part, gain, 0)
                        keep = past if frame < 2 else None
                        side = {0: above, 3: below}.get(row + k)
                        if side is not None:
                            keep = side if keep is None else jnp.logical_and(keep, side)
                        if keep is not None:
                            part = jnp.where(keep, part, 0.0)
                        spread(part.astype(jnp.bfloat16), masks, second, row + k, frame + j)
        pair_weights(plain[1], weights_two)
        offset = bias_two[...]

        def store(block):
            return pltpu.make_async_copy(
                done.at[block], boxes.at[flags[5 + block]], stores.at[block]
            )

        for block in range(RB):
            total = multiply(weights_two, second, 0, block * BF)
            for j in range(BF):
                frame = block * BF + j
                for k in range(2):
                    part = total[k * C : (k + 1) * C, j * W : (j + 1) * W] + offset
                    part = part + raw[frame, k].astype(jnp.float32)
                    part = jnp.where(frame < flags[4], part, 0.0)
                    done[block, j, k] = part.astype(jnp.bfloat16)
            store(block).start()
        for block in range(RB):
            store(block).wait()


def decode(flags, raw, own, sides, tail, tail_sides, weights, vectors, boxes, box_count):
    joined = tail_sides is None
    sides = list(sides) if joined else [*sides, *tail_sides]
    operands = [flags, *vectors, raw, own, *sides[:2], tail, *sides[-2:], *weights]
    specs = [pl.BlockSpec(memory_space=pltpu.SMEM)]
    specs += [pl.BlockSpec(memory_space=pltpu.VMEM)] * (len(operands) - 1)
    aliases = {}
    if boxes is not None:
        aliases = {len(operands): 0}
        operands.append(boxes)
        specs.append(pl.BlockSpec(memory_space=pl.ANY))
    paired = pltpu.VMEM((3, 2 * C, 4 * TAPS), jnp.bfloat16)
    return pl.pallas_call(
        functools.partial(decode_kernel, joined),
        out_shape=jax.ShapeDtypeStruct((box_count, BF, 2, C, W), jnp.bfloat16),
        in_specs=specs,
        out_specs=pl.BlockSpec(memory_space=pl.ANY),
        scratch_shapes=[
            pltpu.VMEM((6 * TAPS, (TAIL + SEG) * W), jnp.bfloat16),
            pltpu.VMEM((4 * TAPS, (2 + SEG) * W), jnp.bfloat16),
            pltpu.VMEM((RB, BF, 2, C, W), jnp.bfloat16),
            paired,
            paired,
            pltpu.SemaphoreType.DMA((RB,)),
        ],
        input_output_aliases=aliases,
        compiler_params=pltpu.CompilerParams(vmem_limit_bytes=32 * 2**20),
        cost_estimate=pl.CostEstimate(flops=6 * 10**9, bytes_accessed=4 * 10**6, transcendentals=0),
        name="decode",
    )(*operands)


def pair_weights(weight, pair):
    pair[:, :C, 3 * TAPS :] = jnp.zeros((3, C, TAPS), jnp.bfloat16)
    pair[:, C:, :TAPS] = jnp.zeros((3, C, TAPS), jnp.bfloat16)
    for tap in range(3):
        for row in range(3):
            for cell in range(3):
                tile = weight[tap, row, cell]
                for k in range(2):
                    start = ((row + k) * 3 + cell) * C
                    pair[tap, k * C : (k + 1) * C, start : start + C] = tile


def local(
    features, frame_counts, places, gain_one, gain_two, conv_one, conv_two, bias_one, bias_two
):
    my_video = lax.axis_index("video")
    my_tm = lax.axis_index("tm")
    my_height = lax.axis_index("height")
    videos = lax.axis_size("video")
    tm_count = lax.axis_size("tm")
    heights = lax.axis_size("height")
    rounds = features.shape[1]

    raw, own = [], []
    for turn in range(rounds):
        segment = features[0, turn]
        if turn > 0:
            segment, own[0] = lax.optimization_barrier((segment, own[0]))
        raw.append(jnp.swapaxes(segment, 1, 2))
        values = raw[turn].astype(jnp.float32)
        own.append(activate(values, gain_one[:, None], 2).astype(jnp.bfloat16))
    past_0, past_1 = (ring(value[SEG - TAIL :], "tm") for value in own)
    sides_0 = neighbours(own[0], "height")
    tail_sides_0 = neighbours(past_0, "height")

    held = lax.dynamic_index_in_dim(
        places.reshape(videos, rounds, tm_count, RB), my_tm, 2, keepdims=False
    )
    mine = lax.dynamic_index_in_dim(held, my_video, 0, keepdims=False)
    count = lax.dynamic_index_in_dim(frame_counts, my_video, 0, keepdims=False)
    owner = mine // (SLOTS * tm_count)
    flags = []
    for turn in range(rounds):
        live = count > turn * tm_count * SEG
        past = jnp.logical_or(turn > 0, my_tm > 0)
        limit = count - (turn * tm_count + my_tm) * SEG
        head = jnp.stack([live, past, my_height > 0, my_height < heights - 1, limit])
        flags.append(jnp.concatenate([head, jnp.minimum(owner[turn], videos - 1)]).astype(jnp.int32))

    wide = [jnp.broadcast_to(v[:, None], (C, W)) for v in (gain_two, bias_one, bias_two)]
    weights = (conv_one, conv_two)
    wanted = (my_video * tm_count + my_tm) * SLOTS + jnp.arange(SLOTS)
    match = (held.reshape(videos, -1)[None] == wanted[:, None, None]).astype(jnp.int32)
    found = jnp.sum(match, axis=(1, 2)) > 0
    source = jnp.sum(match * jnp.arange(videos)[None, :, None], axis=(1, 2))

    arrived = jnp.logical_and(*[side[-1, -1, -1, -1] < jnp.inf for side in sides_0])
    tail_1 = jnp.where(jnp.logical_and(my_tm == 0, arrived), past_0, past_1)
    sides_1 = neighbours(jnp.concatenate([own[1], tail_1]), "height")
    boxes = decode(
        flags[0], raw[0], own[0], sides_0, past_0, tail_sides_0, weights, wide, None, videos
    )
    boxes = decode(flags[1], raw[1], own[1], sides_1, tail_1, None, weights, wide, boxes, videos)
    received = lax.all_to_all(boxes, "video", split_axis=0, concat_axis=0, tiled=True)
    chosen = jnp.take(received, source, axis=0, mode="clip")
    chosen = jnp.where(found[:, None, None, None, None], chosen, jnp.zeros((), jnp.bfloat16))
    return jnp.swapaxes(chosen, 2, 3).reshape(1, SLOTS * BF, C, 2, W)


def solution(mesh):
    placed = (P("video", None, "tm", None, "height", None), P(), P(), P(), P(), P(), P(), P(), P())
    return jax.shard_map(
        local,
        mesh=mesh,
        in_specs=placed,
        out_specs=P("video", "tm", None, "height", None),
        check_vma=False,
    )
```

```python
import functools

import jax
import jax.numpy as jnp
from jax import lax
from jax.experimental import pallas as pl
from jax.experimental.pallas import tpu as pltpu
from jax.sharding import PartitionSpec as P

EPS = 1e-06
BF = 2
RB = 4
SEG = BF * RB
TAIL = 2 * BF
C = 96
W = 128
TAPS = 3 * C
SLOTS = 5


def activate(values, gain, axis):
    mean_square = jnp.mean(values * values, axis=axis, keepdims=True)
    scaled = values * lax.rsqrt(mean_square + EPS) * gain
    return scaled * (0.5 * jnp.tanh(0.5 * scaled) + 0.5)


def ring(value, axis):
    count = lax.axis_size(axis)
    return lax.ppermute(value, axis, [(i, (i + 1) % count) for i in range(count)])


def neighbours(value, axis):
    return ring(value, axis), lax.ppermute(
        value, axis, [((i + 1) % lax.axis_size(axis), i) for i in range(lax.axis_size(axis))]
    )


def spread(values, masks, stack, row, frame):
    left = pltpu.roll(values, 1, 1) * masks[0]
    right = pltpu.roll(values, W - 1, 1) * masks[1]
    columns = slice(frame * W, (frame + 1) * W)
    for tap, shifted in enumerate((left, values, right)):
        start = row * TAPS + tap * C
        stack[start : start + C, columns] = shifted


def multiply(weights, stack, row, frame):
    total = None
    for tap in range(3):
        window = stack[row * TAPS : (row + 4) * TAPS, (frame + tap) * W : (frame + tap + 2) * W]
        part = jnp.dot(weights[tap], window, preferred_element_type=jnp.float32)
        total = part if total is None else total + part
    return total


def decode_kernel(joined, flags, gain_two, bias_one, bias_two, *rest):
    arrays, rest = rest[:9], rest[9:]
    raw, own, low, high, tail, low_tail, high_tail, *plain = arrays
    boxes, first, second, done, weights_one, weights_two, stores = rest[-7:]
    skip = SEG if joined else 0

    @pl.when(flags[0] > 0)
    def _():
        lane = lax.broadcasted_iota(jnp.int32, (C, W), 1)
        masks = [
            jnp.where(lane == edge, 0.0, 1.0).astype(jnp.bfloat16) for edge in (0, W - 1)
        ]
        past = True if joined else flags[1] == 0
        above = flags[2] > 0
        below = flags[3] > 0
        zero = jnp.zeros((), jnp.bfloat16)
        pair_weights(plain[0], weights_one)
        for frames, base, start, parts in (
            (TAIL, 0, skip, (tail, low_tail, high_tail)),
            (SEG, TAIL, 0, (own, low, high)),
        ):
            known = True if base > 0 else past
            for frame in range(frames):
                for row in range(2):
                    values = jnp.where(known, parts[0][start + frame, row], zero)
                    spread(values, masks, first, 2 + row, base + frame)
                    keep = jnp.logical_and(known, above)
                    values = jnp.where(keep, parts[1][start + frame, row], zero)
                    spread(values, masks, first, row, base + frame)
                    keep = jnp.logical_and(known, below)
                    values = jnp.where(keep, parts[2][start + frame, row], zero)
                    spread(values, masks, first, 4 + row, base + frame)
        gain = gain_two[...]
        offset = bias_one[...]
        for row in range(0, 4, 2):
            for frame in range(0, SEG + 2, 2):
                total = multiply(weights_one, first, row, frame)
                for k in range(2):
                    for j in range(2):
                        part = total[k * C : (k + 1) * C, j * W : (j + 1) * W] + offset
                        part = part.astype(jnp.bfloat16).astype(jnp.float32)
                        part = activate(part, gain, 0)
                        keep = past if frame < 2 else None
                        side = {0: above, 3: below}.get(row + k)
                        if side is not None:
                            keep = side if keep is None else jnp.logical_and(keep, side)
                        if keep is not None:
                            part = jnp.where(keep, part, 0.0)
                        spread(part.astype(jnp.bfloat16), masks, second, row + k, frame + j)
        pair_weights(plain[1], weights_two)
        offset = bias_two[...]

        def store(block):
            return pltpu.make_async_copy(
                done.at[block], boxes.at[flags[5 + block]], stores.at[block]
            )

        for block in range(RB):
            total = multiply(weights_two, second, 0, block * BF)
            for j in range(BF):
                frame = block * BF + j
                for k in range(2):
                    part = total[k * C : (k + 1) * C, j * W : (j + 1) * W] + offset
                    part = part + raw[frame, k].astype(jnp.float32)
                    part = jnp.where(frame < flags[4], part, 0.0)
                    done[block, j, k] = part.astype(jnp.bfloat16)
            store(block).start()
        for block in range(RB):
            store(block).wait()


def decode(flags, raw, own, sides, tail, tail_sides, weights, vectors, boxes, box_count):
    joined = tail_sides is None
    sides = list(sides) if joined else [*sides, *tail_sides]
    operands = [flags, *vectors, raw, own, *sides[:2], tail, *sides[-2:], *weights]
    specs = [pl.BlockSpec(memory_space=pltpu.SMEM)]
    specs += [pl.BlockSpec(memory_space=pltpu.VMEM)] * (len(operands) - 1)
    aliases = {}
    if boxes is not None:
        aliases = {len(operands): 0}
        operands.append(boxes)
        specs.append(pl.BlockSpec(memory_space=pl.ANY))
    paired = pltpu.VMEM((3, 2 * C, 4 * TAPS), jnp.bfloat16)
    return pl.pallas_call(
        functools.partial(decode_kernel, joined),
        out_shape=jax.ShapeDtypeStruct((box_count, BF, 2, C, W), jnp.bfloat16),
        in_specs=specs,
        out_specs=pl.BlockSpec(memory_space=pl.ANY),
        scratch_shapes=[
            pltpu.VMEM((6 * TAPS, (TAIL + SEG) * W), jnp.bfloat16),
            pltpu.VMEM((4 * TAPS, (2 + SEG) * W), jnp.bfloat16),
            pltpu.VMEM((RB, BF, 2, C, W), jnp.bfloat16),
            paired,
            paired,
            pltpu.SemaphoreType.DMA((RB,)),
        ],
        input_output_aliases=aliases,
        compiler_params=pltpu.CompilerParams(vmem_limit_bytes=32 * 2**20),
        cost_estimate=pl.CostEstimate(flops=6 * 10**9, bytes_accessed=4 * 10**6, transcendentals=0),
        name="decode",
    )(*operands)


def pair_weights(weight, pair):
    pair[:, :C, 3 * TAPS :] = jnp.zeros((3, C, TAPS), jnp.bfloat16)
    pair[:, C:, :TAPS] = jnp.zeros((3, C, TAPS), jnp.bfloat16)
    for tap in range(3):
        for row in range(3):
            for cell in range(3):
                tile = weight[tap, row, cell]
                for k in range(2):
                    start = ((row + k) * 3 + cell) * C
                    pair[tap, k * C : (k + 1) * C, start : start + C] = tile


def join_kernel(flags, own, last, past, low, high, joined):
    joined[:SEG] = own[...]

    @pl.when(flags[1] > 0)
    def _():
        joined[SEG:] = last[...]

    @pl.when(flags[1] == 0)
    def _():
        joined[SEG:] = past[...]


def join(flags, own, last, past, sides):
    operands = (flags, own, last, past, *sides)
    return pl.pallas_call(
        join_kernel,
        out_shape=jax.ShapeDtypeStruct((SEG + TAIL, 2, C, W), jnp.bfloat16),
        in_specs=[pl.BlockSpec(memory_space=pltpu.SMEM)]
        + [pl.BlockSpec(memory_space=pltpu.VMEM)] * (len(operands) - 1),
        out_specs=pl.BlockSpec(memory_space=pltpu.VMEM),
        compiler_params=pltpu.CompilerParams(vmem_limit_bytes=8 * 2**20),
        name="join",
    )(*operands)


def local(
    features, frame_counts, places, gain_one, gain_two, conv_one, conv_two, bias_one, bias_two
):
    my_video = lax.axis_index("video")
    my_tm = lax.axis_index("tm")
    my_height = lax.axis_index("height")
    videos = lax.axis_size("video")
    tm_count = lax.axis_size("tm")
    heights = lax.axis_size("height")
    rounds = features.shape[1]

    raw, own = [], []
    for turn in range(rounds):
        raw.append(jnp.swapaxes(features[0, turn], 1, 2))
        values = raw[turn].astype(jnp.float32)
        own.append(activate(values, gain_one[:, None], 2).astype(jnp.bfloat16))
    past_0, past_1 = (ring(value[SEG - TAIL :], "tm") for value in own)
    sides_0 = neighbours(own[0], "height")

    held = lax.dynamic_index_in_dim(
        places.reshape(videos, rounds, tm_count, RB), my_tm, 2, keepdims=False
    )
    mine = lax.dynamic_index_in_dim(held, my_video, 0, keepdims=False)
    count = lax.dynamic_index_in_dim(frame_counts, my_video, 0, keepdims=False)
    owner = mine // (SLOTS * tm_count)
    flags = []
    for turn in range(rounds):
        live = count > turn * tm_count * SEG
        leads = my_tm == 0
        limit = count - (turn * tm_count + my_tm) * SEG
        head = jnp.stack([live, leads, my_height > 0, my_height < heights - 1, limit])
        flags.append(jnp.concatenate([head, jnp.minimum(owner[turn], videos - 1)]).astype(jnp.int32))

    wide = [jnp.broadcast_to(v[:, None], (C, W)) for v in (gain_two, bias_one, bias_two)]
    weights = (conv_one, conv_two)
    wanted = (my_video * tm_count + my_tm) * SLOTS + jnp.arange(SLOTS)
    match = (held.reshape(videos, -1)[None] == wanted[:, None, None]).astype(jnp.int32)
    found = jnp.sum(match, axis=(1, 2)) > 0
    source = jnp.sum(match * jnp.arange(videos)[None, :, None], axis=(1, 2))

    past_0, flags, wide, found, source = lax.optimization_barrier(
        (past_0, flags, wide, found, source)
    )
    tail_sides_0 = neighbours(past_0, "height")
    joined = join(flags[1], own[1], past_0, past_1, sides_0)
    sides_1 = neighbours(joined, "height")
    boxes = decode(
        flags[0], raw[0], own[0], sides_0, past_0, tail_sides_0, weights, wide, None, videos
    )
    boxes = decode(flags[1], raw[1], joined, sides_1, joined, None, weights, wide, boxes, videos)
    received = lax.all_to_all(boxes, "video", split_axis=0, concat_axis=0, tiled=True)
    chosen = jnp.take(received, source, axis=0, mode="clip")
    chosen = jnp.where(found[:, None, None, None, None], chosen, jnp.zeros((), jnp.bfloat16))
    return jnp.swapaxes(chosen, 2, 3).reshape(1, SLOTS * BF, C, 2, W)


def solution(mesh):
    placed = (P("video", None, "tm", None, "height", None), P(), P(), P(), P(), P(), P(), P(), P())
    return jax.shard_map(
        local,
        mesh=mesh,
        in_specs=placed,
        out_specs=P("video", "tm", None, "height", None),
        check_vma=False,
    )
```

```python
import functools

import jax
import jax.numpy as jnp
from jax import lax
from jax.experimental import pallas as pl
from jax.experimental.pallas import tpu as pltpu
from jax.sharding import PartitionSpec as P

EPS = 1e-06
BF = 2
RB = 4
SEG = BF * RB
TAIL = 2 * BF
C = 96
W = 128
TAPS = 3 * C
SLOTS = 5


def activate(values, gain, axis):
    mean_square = jnp.mean(values * values, axis=axis, keepdims=True)
    scaled = values * lax.rsqrt(mean_square + EPS) * gain
    return scaled * (0.5 * jnp.tanh(0.5 * scaled) + 0.5)


def ring(value, axis):
    count = lax.axis_size(axis)
    return lax.ppermute(value, axis, [(i, (i + 1) % count) for i in range(count)])


def neighbours(value, axis):
    return ring(value, axis), lax.ppermute(
        value, axis, [((i + 1) % lax.axis_size(axis), i) for i in range(lax.axis_size(axis))]
    )


def spread(values, masks, stack, row, frame):
    left = pltpu.roll(values, 1, 1) * masks[0]
    right = pltpu.roll(values, W - 1, 1) * masks[1]
    columns = slice(frame * W, (frame + 1) * W)
    for tap, shifted in enumerate((left, values, right)):
        start = row * TAPS + tap * C
        stack[start : start + C, columns] = shifted


def convolve(weights, stack, row, frames, sums):
    last = frames // 2
    for pair in range(last + 1):
        window = stack[row * TAPS : (row + 3) * TAPS, 2 * pair * W : (2 * pair + 2) * W]
        low, high = (0 if pair < last else 1), (3 if pair > 0 else 2)
        parts = jnp.dot(
            weights[low * C : high * C, :], window, preferred_element_type=jnp.float32
        )
        parts = {tap: parts[(tap - low) * C :][:C] for tap in range(low, high)}
        if 0 in parts:
            sums[row, :, 2 * pair * W : (2 * pair + 2) * W] = parts[0]
        for j in range(2):
            frame = 2 * pair + j - 1
            if 0 <= frame < frames:
                columns = slice(frame * W, (frame + 1) * W)
                sums[row, :, columns] = sums[row, :, columns] + parts[1][:, j * W : (j + 1) * W]
        if 2 in parts:
            yield 2 * pair - 2, sums[row, :, (2 * pair - 2) * W : 2 * pair * W] + parts[2]


def decode_kernel(joined, flags, gain_two, bias_one, bias_two, *rest):
    arrays, rest = rest[:9], rest[9:]
    raw, own, low, high, tail, low_tail, high_tail, *plain = arrays
    boxes, first, second, sums, done, weights_one, weights_two, stores = rest[-8:]
    skip = SEG if joined else 0

    @pl.when(flags[0] > 0)
    def _():
        lane = lax.broadcasted_iota(jnp.int32, (C, W), 1)
        masks = [
            jnp.where(lane == edge, 0.0, 1.0).astype(jnp.bfloat16) for edge in (0, W - 1)
        ]
        past = True if joined else flags[1] == 0
        above = flags[2] > 0
        below = flags[3] > 0
        zero = jnp.zeros((), jnp.bfloat16)
        lay_out(plain[0], weights_one)
        def fill(row):
            part, at = row // 2, row % 2
            side = {0: above, 2: below}.get(part)
            for frame in range(TAIL + SEG):
                if frame < TAIL:
                    values = (low_tail, tail, high_tail)[part][skip + frame, at]
                    keep = past
                else:
                    values = (low, own, high)[part][frame - TAIL, at]
                    keep = None
                if side is not None:
                    keep = side if keep is None else jnp.logical_and(keep, side)
                if keep is not None:
                    values = jnp.where(keep, values, zero)
                spread(values, masks, first, row, frame)

        gain = gain_two[...]
        offset_one = bias_one[...]
        offset_two = bias_two[...]

        def inner(row):
            for frame, total in convolve(weights_one, first, row, SEG + 2, sums):
                for j in range(2):
                    part = total[:, j * W : (j + 1) * W] + offset_one
                    part = part.astype(jnp.bfloat16).astype(jnp.float32)
                    part = activate(part, gain, 0)
                    keep = past if frame < 2 else None
                    side = {0: above, 3: below}.get(row)
                    if side is not None:
                        keep = side if keep is None else jnp.logical_and(keep, side)
                    if keep is not None:
                        part = jnp.where(keep, part, 0.0)
                    spread(part.astype(jnp.bfloat16), masks, second, row, frame + j)

        def store(block):
            return pltpu.make_async_copy(
                done.at[block], boxes.at[flags[5 + block]], stores.at[block]
            )

        def outer(row):
            for start, total in convolve(weights_two, second, row, SEG, sums):
                for j in range(BF):
                    part = total[:, j * W : (j + 1) * W] + offset_two
                    part = part + raw[start + j, row].astype(jnp.float32)
                    part = jnp.where(start + j < flags[4], part, 0.0)
                    done[start // BF, j, row] = part.astype(jnp.bfloat16)
                if row == 1:
                    store(start // BF).start()

        for row in range(3):
            fill(row)
        inner(0)
        fill(3)
        inner(1)
        fill(4)
        lay_out(plain[1], weights_two)
        inner(2)
        fill(5)
        outer(0)
        inner(3)
        outer(1)
        for block in range(RB):
            store(block).wait()


def decode(flags, raw, own, sides, tail, tail_sides, weights, vectors, boxes, box_count):
    joined = tail_sides is None
    sides = list(sides) if joined else [*sides, *tail_sides]
    operands = [flags, *vectors, raw, own, *sides[:2], tail, *sides[-2:], *weights]
    specs = [pl.BlockSpec(memory_space=pltpu.SMEM)]
    specs += [pl.BlockSpec(memory_space=pltpu.VMEM)] * (len(operands) - 1)
    aliases = {}
    if boxes is not None:
        aliases = {len(operands): 0}
        operands.append(boxes)
        specs.append(pl.BlockSpec(memory_space=pl.ANY))
    taps = pltpu.VMEM((3 * C, 3 * TAPS), jnp.bfloat16)
    return pl.pallas_call(
        functools.partial(decode_kernel, joined),
        out_shape=jax.ShapeDtypeStruct((box_count, BF, 2, C, W), jnp.bfloat16),
        in_specs=specs,
        out_specs=pl.BlockSpec(memory_space=pl.ANY),
        scratch_shapes=[
            pltpu.VMEM((6 * TAPS, (TAIL + SEG) * W), jnp.bfloat16),
            pltpu.VMEM((4 * TAPS, (2 + SEG) * W), jnp.bfloat16),
            pltpu.VMEM((4, C, (2 + SEG) * W), jnp.float32),
            pltpu.VMEM((RB, BF, 2, C, W), jnp.bfloat16),
            taps,
            taps,
            pltpu.SemaphoreType.DMA((RB,)),
        ],
        input_output_aliases=aliases,
        compiler_params=pltpu.CompilerParams(vmem_limit_bytes=32 * 2**20),
        cost_estimate=pl.CostEstimate(flops=6 * 10**9, bytes_accessed=4 * 10**6, transcendentals=0),
        name="decode",
    )(*operands)


def lay_out(weight, rows):
    for tap in range(3):
        for row in range(3):
            for cell in range(3):
                start = (row * 3 + cell) * C
                rows[tap * C : (tap + 1) * C, start : start + C] = weight[tap, row, cell]


def join_kernel(flags, own, last, past, low, high, joined):
    joined[:SEG] = own[...]

    @pl.when(flags[1] > 0)
    def _():
        joined[SEG:] = last[...]

    @pl.when(flags[1] == 0)
    def _():
        joined[SEG:] = past[...]


def join(flags, own, last, past, sides):
    operands = (flags, own, last, past, *sides)
    return pl.pallas_call(
        join_kernel,
        out_shape=jax.ShapeDtypeStruct((SEG + TAIL, 2, C, W), jnp.bfloat16),
        in_specs=[pl.BlockSpec(memory_space=pltpu.SMEM)]
        + [pl.BlockSpec(memory_space=pltpu.VMEM)] * (len(operands) - 1),
        out_specs=pl.BlockSpec(memory_space=pltpu.VMEM),
        compiler_params=pltpu.CompilerParams(vmem_limit_bytes=8 * 2**20),
        name="join",
    )(*operands)


def local(
    features, frame_counts, places, gain_one, gain_two, conv_one, conv_two, bias_one, bias_two
):
    my_video = lax.axis_index("video")
    my_tm = lax.axis_index("tm")
    my_height = lax.axis_index("height")
    videos = lax.axis_size("video")
    tm_count = lax.axis_size("tm")
    heights = lax.axis_size("height")
    rounds = features.shape[1]

    raw, own = [], []
    for turn in range(rounds):
        raw.append(jnp.swapaxes(features[0, turn], 1, 2))
        values = raw[turn].astype(jnp.float32)
        own.append(activate(values, gain_one[:, None], 2).astype(jnp.bfloat16))
    past_0, past_1 = (ring(value[SEG - TAIL :], "tm") for value in own)
    sides_0 = neighbours(own[0], "height")

    held = lax.dynamic_index_in_dim(
        places.reshape(videos, rounds, tm_count, RB), my_tm, 2, keepdims=False
    )
    mine = lax.dynamic_index_in_dim(held, my_video, 0, keepdims=False)
    count = lax.dynamic_index_in_dim(frame_counts, my_video, 0, keepdims=False)
    owner = mine // (SLOTS * tm_count)
    flags = []
    for turn in range(rounds):
        live = count > turn * tm_count * SEG
        leads = my_tm == 0
        limit = count - (turn * tm_count + my_tm) * SEG
        head = jnp.stack([live, leads, my_height > 0, my_height < heights - 1, limit])
        flags.append(jnp.concatenate([head, jnp.minimum(owner[turn], videos - 1)]).astype(jnp.int32))

    wide = [jnp.broadcast_to(v[:, None], (C, W)) for v in (gain_two, bias_one, bias_two)]
    weights = (conv_one, conv_two)
    wanted = (my_video * tm_count + my_tm) * SLOTS + jnp.arange(SLOTS)
    match = (held.reshape(videos, -1)[None] == wanted[:, None, None]).astype(jnp.int32)
    found = jnp.sum(match, axis=(1, 2)) > 0
    source = jnp.sum(match * jnp.arange(videos)[None, :, None], axis=(1, 2))

    past_0, flags, wide, found, source = lax.optimization_barrier(
        (past_0, flags, wide, found, source)
    )
    tail_sides_0 = neighbours(past_0, "height")
    joined = join(flags[1], own[1], past_0, past_1, sides_0)
    sides_1 = neighbours(joined, "height")
    boxes = decode(
        flags[0], raw[0], own[0], sides_0, past_0, tail_sides_0, weights, wide, None, videos
    )
    boxes = decode(flags[1], raw[1], joined, sides_1, joined, None, weights, wide, boxes, videos)
    received = lax.all_to_all(boxes, "video", split_axis=0, concat_axis=0, tiled=True)
    chosen = jnp.take(received, source, axis=0, mode="clip")
    chosen = jnp.where(found[:, None, None, None, None], chosen, jnp.zeros((), jnp.bfloat16))
    return jnp.swapaxes(chosen, 2, 3).reshape(1, SLOTS * BF, C, 2, W)


def solution(mesh):
    placed = (P("video", None, "tm", None, "height", None), P(), P(), P(), P(), P(), P(), P(), P())
    return jax.shard_map(
        local,
        mesh=mesh,
        in_specs=placed,
        out_specs=P("video", "tm", None, "height", None),
        check_vma=False,
    )
```

```python
import functools

import jax
import jax.numpy as jnp
from jax import lax
from jax.experimental import pallas as pl
from jax.experimental.pallas import tpu as pltpu
from jax.sharding import PartitionSpec as P

EPS = 1e-06
BF = 2
RB = 4
SEG = BF * RB
TAIL = 2 * BF
C = 96
W = 128
TAPS = 3 * C
SLOTS = 5


def activate(values, gain, axis):
    mean_square = jnp.mean(values * values, axis=axis, keepdims=True)
    scaled = values * lax.rsqrt(mean_square + EPS) * gain
    return scaled * (0.5 * jnp.tanh(0.5 * scaled) + 0.5)


def ring(value, axis):
    count = lax.axis_size(axis)
    return lax.ppermute(value, axis, [(i, (i + 1) % count) for i in range(count)])


def neighbours(value, axis):
    return ring(value, axis), lax.ppermute(
        value, axis, [((i + 1) % lax.axis_size(axis), i) for i in range(lax.axis_size(axis))]
    )


def spread(values, masks, stack, row, frame):
    left = pltpu.roll(values, 1, 1) * masks[0]
    right = pltpu.roll(values, W - 1, 1) * masks[1]
    columns = slice(frame * W, (frame + 1) * W)
    for tap, shifted in enumerate((left, values, right)):
        start = row * TAPS + tap * C
        stack[start : start + C, columns] = shifted


def convolve(weights, stack, row, frames, sums):
    last = frames // 2
    for pair in range(last + 1):
        window = stack[row * TAPS : (row + 3) * TAPS, 2 * pair * W : (2 * pair + 2) * W]
        low, high = (0 if pair < last else 1), (3 if pair > 0 else 2)
        parts = jnp.dot(
            weights[low * C : high * C, :], window, preferred_element_type=jnp.float32
        )
        parts = {tap: parts[(tap - low) * C :][:C] for tap in range(low, high)}
        if 0 in parts:
            sums[row, :, 2 * pair * W : (2 * pair + 2) * W] = parts[0]
        for j in range(2):
            frame = 2 * pair + j - 1
            if 0 <= frame < frames:
                columns = slice(frame * W, (frame + 1) * W)
                sums[row, :, columns] = sums[row, :, columns] + parts[1][:, j * W : (j + 1) * W]
        if 2 in parts:
            yield 2 * pair - 2, sums[row, :, (2 * pair - 2) * W : 2 * pair * W] + parts[2]


def decode_kernel(joined, flags, gain_two, bias_one, bias_two, *rest):
    arrays, rest = rest[:9], rest[9:]
    raw, own, low, high, tail, low_tail, high_tail, *weights = arrays
    if joined:
        weights_one, weights_two = weights
        boxes, first, second, sums, done, stores = rest[-6:]
    else:
        boxes, weights_one, weights_two, first, second, sums, done, stores = rest[-8:]
    skip = SEG if joined else 0

    @pl.when(flags[0] > 0)
    def _():
        lane = lax.broadcasted_iota(jnp.int32, (C, W), 1)
        masks = [
            jnp.where(lane == edge, 0.0, 1.0).astype(jnp.bfloat16) for edge in (0, W - 1)
        ]
        past = True if joined else flags[1] == 0
        above = flags[2] > 0
        below = flags[3] > 0
        zero = jnp.zeros((), jnp.bfloat16)
        if not joined:
            lay_out(weights[0], weights_one)
        def fill(row):
            part, at = row // 2, row % 2
            side = {0: above, 2: below}.get(part)
            for frame in range(TAIL + SEG):
                if frame < TAIL:
                    values = (low_tail, tail, high_tail)[part][skip + frame, at]
                    keep = past
                else:
                    values = (low, own, high)[part][frame - TAIL, at]
                    keep = None
                if side is not None:
                    keep = side if keep is None else jnp.logical_and(keep, side)
                if keep is not None:
                    values = jnp.where(keep, values, zero)
                spread(values, masks, first, row, frame)

        gain = gain_two[...]
        offset_one = bias_one[...]
        offset_two = bias_two[...]

        def inner(row):
            for frame, total in convolve(weights_one, first, row, SEG + 2, sums):
                for j in range(2):
                    part = total[:, j * W : (j + 1) * W] + offset_one
                    part = part.astype(jnp.bfloat16).astype(jnp.float32)
                    part = activate(part, gain, 0)
                    keep = past if frame < 2 else None
                    side = {0: above, 3: below}.get(row)
                    if side is not None:
                        keep = side if keep is None else jnp.logical_and(keep, side)
                    if keep is not None:
                        part = jnp.where(keep, part, 0.0)
                    spread(part.astype(jnp.bfloat16), masks, second, row, frame + j)

        def store(block):
            return pltpu.make_async_copy(
                done.at[block], boxes.at[flags[5 + block]], stores.at[block]
            )

        def outer(row):
            for start, total in convolve(weights_two, second, row, SEG, sums):
                for j in range(BF):
                    part = total[:, j * W : (j + 1) * W] + offset_two
                    part = part + raw[start + j, row].astype(jnp.float32)
                    part = jnp.where(start + j < flags[4], part, 0.0)
                    done[start // BF, j, row] = part.astype(jnp.bfloat16)
                if row == 1:
                    store(start // BF).start()

        for row in range(3):
            fill(row)
        inner(0)
        fill(3)
        inner(1)
        fill(4)
        if not joined:
            lay_out(weights[1], weights_two)
        inner(2)
        fill(5)
        outer(0)
        inner(3)
        outer(1)
        for block in range(RB):
            store(block).wait()


def decode(flags, raw, own, sides, tail, tail_sides, weights, vectors, boxes, box_count):
    joined = tail_sides is None
    sides = list(sides) if joined else [*sides, *tail_sides]
    operands = [flags, *vectors, raw, own, *sides[:2], tail, *sides[-2:], *weights]
    specs = [pl.BlockSpec(memory_space=pltpu.SMEM)]
    specs += [pl.BlockSpec(memory_space=pltpu.VMEM)] * (len(operands) - 1)
    aliases = {}
    if boxes is not None:
        aliases = {len(operands): 0}
        operands.append(boxes)
        specs.append(pl.BlockSpec(memory_space=pl.ANY))
    taps = jax.ShapeDtypeStruct((3 * C, 3 * TAPS), jnp.bfloat16)
    shape = jax.ShapeDtypeStruct((box_count, BF, 2, C, W), jnp.bfloat16)
    inside = pl.BlockSpec(memory_space=pltpu.VMEM)
    outside = pl.BlockSpec(memory_space=pl.ANY)
    return pl.pallas_call(
        functools.partial(decode_kernel, joined),
        out_shape=shape if joined else (shape, taps, taps),
        in_specs=specs,
        out_specs=outside if joined else (outside, inside, inside),
        scratch_shapes=[
            pltpu.VMEM((6 * TAPS, (TAIL + SEG) * W), jnp.bfloat16),
            pltpu.VMEM((4 * TAPS, (2 + SEG) * W), jnp.bfloat16),
            pltpu.VMEM((4, C, (2 + SEG) * W), jnp.float32),
            pltpu.VMEM((RB, BF, 2, C, W), jnp.bfloat16),
            pltpu.SemaphoreType.DMA((RB,)),
        ],
        input_output_aliases=aliases,
        compiler_params=pltpu.CompilerParams(vmem_limit_bytes=32 * 2**20),
        cost_estimate=pl.CostEstimate(flops=6 * 10**9, bytes_accessed=4 * 10**6, transcendentals=0),
        name="decode",
    )(*operands)


def lay_out(weight, rows):
    for tap in range(3):
        for row in range(3):
            for cell in range(3):
                start = (row * 3 + cell) * C
                rows[tap * C : (tap + 1) * C, start : start + C] = weight[tap, row, cell]


def join_kernel(flags, own, last, past, low, high, joined):
    joined[:SEG] = own[...]

    @pl.when(flags[1] > 0)
    def _():
        joined[SEG:] = last[...]

    @pl.when(flags[1] == 0)
    def _():
        joined[SEG:] = past[...]


def join(flags, own, last, past, sides):
    operands = (flags, own, last, past, *sides)
    return pl.pallas_call(
        join_kernel,
        out_shape=jax.ShapeDtypeStruct((SEG + TAIL, 2, C, W), jnp.bfloat16),
        in_specs=[pl.BlockSpec(memory_space=pltpu.SMEM)]
        + [pl.BlockSpec(memory_space=pltpu.VMEM)] * (len(operands) - 1),
        out_specs=pl.BlockSpec(memory_space=pltpu.VMEM),
        compiler_params=pltpu.CompilerParams(vmem_limit_bytes=8 * 2**20),
        name="join",
    )(*operands)


def local(
    features, frame_counts, places, gain_one, gain_two, conv_one, conv_two, bias_one, bias_two
):
    my_video = lax.axis_index("video")
    my_tm = lax.axis_index("tm")
    my_height = lax.axis_index("height")
    videos = lax.axis_size("video")
    tm_count = lax.axis_size("tm")
    heights = lax.axis_size("height")
    rounds = features.shape[1]

    raw, own = [], []
    for turn in range(rounds):
        if turn > 0:
            features, own[0] = lax.optimization_barrier((features, own[0]))
        raw.append(jnp.swapaxes(features[0, turn], 1, 2))
        values = raw[turn].astype(jnp.float32)
        own.append(activate(values, gain_one[:, None], 2).astype(jnp.bfloat16))
    past_1 = ring(own[1][SEG - TAIL :], "tm")
    sides_0 = neighbours(own[0], "height")
    past_0 = ring(own[0][SEG - TAIL :], "tm")

    held = lax.dynamic_index_in_dim(
        places.reshape(videos, rounds, tm_count, RB), my_tm, 2, keepdims=False
    )
    mine = lax.dynamic_index_in_dim(held, my_video, 0, keepdims=False)
    count = lax.dynamic_index_in_dim(frame_counts, my_video, 0, keepdims=False)
    owner = mine // (SLOTS * tm_count)
    flags = []
    for turn in range(rounds):
        live = count > turn * tm_count * SEG
        leads = my_tm == 0
        limit = count - (turn * tm_count + my_tm) * SEG
        head = jnp.stack([live, leads, my_height > 0, my_height < heights - 1, limit])
        flags.append(jnp.concatenate([head, jnp.minimum(owner[turn], videos - 1)]).astype(jnp.int32))

    wide = [jnp.broadcast_to(v[:, None], (C, W)) for v in (gain_two, bias_one, bias_two)]
    weights = (conv_one, conv_two)
    wanted = (my_video * tm_count + my_tm) * SLOTS + jnp.arange(SLOTS)
    match = (held.reshape(videos, -1)[None] == wanted[:, None, None]).astype(jnp.int32)
    found = jnp.sum(match, axis=(1, 2)) > 0
    source = jnp.sum(match * jnp.arange(videos)[None, :, None], axis=(1, 2))

    past_0, flags, wide, found, source = lax.optimization_barrier(
        (past_0, flags, wide, found, source)
    )
    tail_sides_0 = neighbours(past_0, "height")
    joined = join(flags[1], own[1], past_0, past_1, sides_0)
    sides_1 = neighbours(joined, "height")
    boxes, *weights = decode(
        flags[0], raw[0], own[0], sides_0, past_0, tail_sides_0, weights, wide, None, videos
    )
    boxes = decode(flags[1], raw[1], joined, sides_1, joined, None, weights, wide, boxes, videos)
    received = lax.all_to_all(boxes, "video", split_axis=0, concat_axis=0, tiled=True)
    chosen = jnp.take(received, source, axis=0, mode="clip")
    chosen = jnp.where(found[:, None, None, None, None], chosen, jnp.zeros((), jnp.bfloat16))
    return jnp.swapaxes(chosen, 2, 3).reshape(1, SLOTS * BF, C, 2, W)


def solution(mesh):
    placed = (P("video", None, "tm", None, "height", None), P(), P(), P(), P(), P(), P(), P(), P())
    return jax.shard_map(
        local,
        mesh=mesh,
        in_specs=placed,
        out_specs=P("video", "tm", None, "height", None),
        check_vma=False,
    )
```

```python
import functools

import jax
import jax.numpy as jnp
from jax import lax
from jax.experimental import pallas as pl
from jax.experimental.pallas import tpu as pltpu
from jax.sharding import PartitionSpec as P

EPS = 1e-06
BF = 2
RB = 4
SEG = BF * RB
TAIL = 2 * BF
C = 96
W = 128
TAPS = 3 * C
SLOTS = 5


def activate(values, gain, axis):
    mean_square = jnp.mean(values * values, axis=axis, keepdims=True)
    scaled = values * lax.rsqrt(mean_square + EPS) * gain
    return scaled * (0.5 * jnp.tanh(0.5 * scaled) + 0.5)


def ring(value, axis):
    count = lax.axis_size(axis)
    return lax.ppermute(value, axis, [(i, (i + 1) % count) for i in range(count)])


def neighbours(value, axis):
    return ring(value, axis), lax.ppermute(
        value, axis, [((i + 1) % lax.axis_size(axis), i) for i in range(lax.axis_size(axis))]
    )


def spread(values, masks, stack, row, frame):
    left = pltpu.roll(values, 1, 1) * masks[0]
    right = pltpu.roll(values, W - 1, 1) * masks[1]
    columns = slice(frame * W, (frame + 1) * W)
    for tap, shifted in enumerate((left, values, right)):
        start = row * TAPS + tap * C
        stack[start : start + C, columns] = shifted


def convolve(weights, stack, row, frames, sums):
    last = frames // 2
    for pair in range(last + 1):
        window = stack[row * TAPS : (row + 3) * TAPS, 2 * pair * W : (2 * pair + 2) * W]
        low, high = (0 if pair < last else 1), (3 if pair > 0 else 2)
        parts = jnp.dot(
            weights[low * C : high * C, :], window, preferred_element_type=jnp.float32
        )
        parts = {tap: parts[(tap - low) * C :][:C] for tap in range(low, high)}
        if 0 in parts:
            sums[row, :, 2 * pair * W : (2 * pair + 2) * W] = parts[0]
        for j in range(2):
            frame = 2 * pair + j - 1
            if 0 <= frame < frames:
                columns = slice(frame * W, (frame + 1) * W)
                sums[row, :, columns] = sums[row, :, columns] + parts[1][:, j * W : (j + 1) * W]
        if 2 in parts:
            yield 2 * pair - 2, sums[row, :, (2 * pair - 2) * W : 2 * pair * W] + parts[2]


def decode_kernel(joined, flags, gain_two, bias_one, bias_two, *rest):
    arrays, rest = rest[:9], rest[9:]
    raw, own, low, high, tail, low_tail, high_tail, *weights = arrays
    if joined:
        weights_one, weights_two = weights
        boxes, first, second, sums, done, stores = rest[-6:]
    else:
        boxes, weights_one, weights_two, first, second, sums, done, stores = rest[-8:]
    skip = SEG if joined else 0

    @pl.when(flags[0] > 0)
    def _():
        lane = lax.broadcasted_iota(jnp.int32, (C, W), 1)
        masks = [
            jnp.where(lane == edge, 0.0, 1.0).astype(jnp.bfloat16) for edge in (0, W - 1)
        ]
        past = True if joined else flags[1] == 0
        above = flags[2] > 0
        below = flags[3] > 0
        zero = jnp.zeros((), jnp.bfloat16)
        if not joined:
            lay_out(weights[0], weights_one)
        def fill(row):
            part, at = row // 2, row % 2
            side = {0: above, 2: below}.get(part)
            for frame in range(TAIL + SEG):
                if frame < TAIL:
                    values = (low_tail, tail, high_tail)[part][skip + frame, at]
                    keep = past
                else:
                    values = (low, own, high)[part][frame - TAIL, at]
                    keep = None
                if side is not None:
                    keep = side if keep is None else jnp.logical_and(keep, side)
                if keep is not None:
                    values = jnp.where(keep, values, zero)
                spread(values, masks, first, row, frame)

        gain = gain_two[...]
        offset_one = bias_one[...]
        offset_two = bias_two[...]

        def inner(row):
            for frame, total in convolve(weights_one, first, row, SEG + 2, sums):
                for j in range(2):
                    part = total[:, j * W : (j + 1) * W] + offset_one
                    part = part.astype(jnp.bfloat16).astype(jnp.float32)
                    part = activate(part, gain, 0)
                    keep = past if frame < 2 else None
                    side = {0: above, 3: below}.get(row)
                    if side is not None:
                        keep = side if keep is None else jnp.logical_and(keep, side)
                    if keep is not None:
                        part = jnp.where(keep, part, 0.0)
                    spread(part.astype(jnp.bfloat16), masks, second, row, frame + j)

        def store(block):
            return pltpu.make_async_copy(
                done.at[block], boxes.at[flags[5 + block]], stores.at[block]
            )

        def outer(row):
            for start, total in convolve(weights_two, second, row, SEG, sums):
                for j in range(BF):
                    part = total[:, j * W : (j + 1) * W] + offset_two
                    part = part + raw[start + j, row].astype(jnp.float32)
                    part = jnp.where(start + j < flags[4], part, 0.0)
                    done[start // BF, j, row] = part.astype(jnp.bfloat16)
                if row == 1:
                    store(start // BF).start()

        for row in range(3):
            fill(row)
        inner(0)
        fill(3)
        inner(1)
        fill(4)
        if not joined:
            lay_out(weights[1], weights_two)
        inner(2)
        fill(5)
        outer(0)
        inner(3)
        outer(1)
        for block in range(RB):
            store(block).wait()


def decode(flags, raw, own, sides, tail, tail_sides, weights, vectors, boxes, box_count):
    joined = tail_sides is None
    sides = list(sides) if joined else [*sides, *tail_sides]
    operands = [flags, *vectors, raw, own, *sides[:2], tail, *sides[-2:], *weights]
    specs = [pl.BlockSpec(memory_space=pltpu.SMEM)]
    specs += [pl.BlockSpec(memory_space=pltpu.VMEM)] * (len(operands) - 1)
    aliases = {}
    if boxes is not None:
        aliases = {len(operands): 0}
        operands.append(boxes)
        specs.append(pl.BlockSpec(memory_space=pl.ANY))
    taps = jax.ShapeDtypeStruct((3 * C, 3 * TAPS), jnp.bfloat16)
    shape = jax.ShapeDtypeStruct((box_count, BF, 2, C, W), jnp.bfloat16)
    inside = pl.BlockSpec(memory_space=pltpu.VMEM)
    outside = pl.BlockSpec(memory_space=pl.ANY)
    return pl.pallas_call(
        functools.partial(decode_kernel, joined),
        out_shape=shape if joined else (shape, taps, taps),
        in_specs=specs,
        out_specs=outside if joined else (outside, inside, inside),
        scratch_shapes=[
            pltpu.VMEM((6 * TAPS, (TAIL + SEG) * W), jnp.bfloat16),
            pltpu.VMEM((4 * TAPS, (2 + SEG) * W), jnp.bfloat16),
            pltpu.VMEM((4, C, (2 + SEG) * W), jnp.float32),
            pltpu.VMEM((RB, BF, 2, C, W), jnp.bfloat16),
            pltpu.SemaphoreType.DMA((RB,)),
        ],
        input_output_aliases=aliases,
        compiler_params=pltpu.CompilerParams(vmem_limit_bytes=32 * 2**20),
        cost_estimate=pl.CostEstimate(flops=6 * 10**9, bytes_accessed=4 * 10**6, transcendentals=0),
        name="decode",
    )(*operands)


def lay_out(weight, rows):
    for tap in range(3):
        for row in range(3):
            for cell in range(3):
                start = (row * 3 + cell) * C
                rows[tap * C : (tap + 1) * C, start : start + C] = weight[tap, row, cell]


def join_kernel(flags, own, last, past, low, high, joined):
    joined[:SEG] = own[...]

    @pl.when(flags[1] > 0)
    def _():
        joined[SEG:] = last[...]

    @pl.when(flags[1] == 0)
    def _():
        joined[SEG:] = past[...]


def join(flags, own, last, past, sides):
    operands = (flags, own, last, past, *sides)
    return pl.pallas_call(
        join_kernel,
        out_shape=jax.ShapeDtypeStruct((SEG + TAIL, 2, C, W), jnp.bfloat16),
        in_specs=[pl.BlockSpec(memory_space=pltpu.SMEM)]
        + [pl.BlockSpec(memory_space=pltpu.VMEM)] * (len(operands) - 1),
        out_specs=pl.BlockSpec(memory_space=pltpu.VMEM),
        compiler_params=pltpu.CompilerParams(vmem_limit_bytes=8 * 2**20),
        name="join",
    )(*operands)


def local(
    features, frame_counts, places, gain_one, gain_two, conv_one, conv_two, bias_one, bias_two
):
    my_video = lax.axis_index("video")
    my_tm = lax.axis_index("tm")
    my_height = lax.axis_index("height")
    videos = lax.axis_size("video")
    tm_count = lax.axis_size("tm")
    heights = lax.axis_size("height")
    rounds = features.shape[1]

    raw, own = [], []
    for turn in range(rounds):
        raw.append(jnp.swapaxes(features[0, turn], 1, 2))
        values = raw[turn].astype(jnp.float32)
        own.append(activate(values, gain_one[:, None], 2).astype(jnp.bfloat16))
    past_0, past_1 = (ring(value[SEG - TAIL :], "tm") for value in own)
    sides_0 = neighbours(own[0], "height")

    held = lax.dynamic_index_in_dim(
        places.reshape(videos, rounds, tm_count, RB), my_tm, 2, keepdims=False
    )
    mine = lax.dynamic_index_in_dim(held, my_video, 0, keepdims=False)
    count = lax.dynamic_index_in_dim(frame_counts, my_video, 0, keepdims=False)
    owner = mine // (SLOTS * tm_count)
    flags = []
    for turn in range(rounds):
        live = count > turn * tm_count * SEG
        leads = my_tm == 0
        limit = count - (turn * tm_count + my_tm) * SEG
        head = jnp.stack([live, leads, my_height > 0, my_height < heights - 1, limit])
        flags.append(jnp.concatenate([head, jnp.minimum(owner[turn], videos - 1)]).astype(jnp.int32))

    wide = [jnp.broadcast_to(v[:, None], (C, W)) for v in (gain_two, bias_one, bias_two)]
    weights = (conv_one, conv_two)
    wanted = (my_video * tm_count + my_tm) * SLOTS + jnp.arange(SLOTS)
    match = (held.reshape(videos, -1)[None] == wanted[:, None, None]).astype(jnp.int32)
    found = jnp.sum(match, axis=(1, 2)) > 0
    source = jnp.sum(match * jnp.arange(videos)[None, :, None], axis=(1, 2))

    past_0, flags, wide, found, source = lax.optimization_barrier(
        (past_0, flags, wide, found, source)
    )
    tail_sides_0 = neighbours(past_0, "height")
    joined = join(flags[1], own[1], past_0, past_1, sides_0)
    sides_1 = neighbours(joined, "height")
    boxes, *weights = decode(
        flags[0], raw[0], own[0], sides_0, past_0, tail_sides_0, weights, wide, None, videos
    )
    boxes = decode(flags[1], raw[1], joined, sides_1, joined, None, weights, wide, boxes, videos)
    received = lax.all_to_all(boxes, "video", split_axis=0, concat_axis=0, tiled=True)
    chosen = jnp.take(received, source, axis=0, mode="clip")
    chosen = jnp.where(found[:, None, None, None, None], chosen, jnp.zeros((), jnp.bfloat16))
    return jnp.swapaxes(chosen, 2, 3).reshape(1, SLOTS * BF, C, 2, W)


def solution(mesh):
    placed = (P("video", None, "tm", None, "height", None), P(), P(), P(), P(), P(), P(), P(), P())
    return jax.shard_map(
        local,
        mesh=mesh,
        in_specs=placed,
        out_specs=P("video", "tm", None, "height", None),
        check_vma=False,
    )
```

```python
import functools

import jax
import jax.numpy as jnp
from jax import lax
from jax.experimental import pallas as pl
from jax.experimental.pallas import tpu as pltpu
from jax.sharding import PartitionSpec as P

EPS = 1e-06
BF = 2
RB = 4
SEG = BF * RB
TAIL = 2 * BF
C = 96
W = 128
TAPS = 3 * C
SLOTS = 5


def activate(values, gain, axis):
    mean_square = jnp.mean(values * values, axis=axis, keepdims=True)
    scaled = values * lax.rsqrt(mean_square + EPS) * gain
    return scaled * (0.5 * jnp.tanh(0.5 * scaled) + 0.5)


def ring(value, axis):
    count = lax.axis_size(axis)
    return lax.ppermute(value, axis, [(i, (i + 1) % count) for i in range(count)])


def neighbours(value, axis):
    return ring(value, axis), lax.ppermute(
        value, axis, [((i + 1) % lax.axis_size(axis), i) for i in range(lax.axis_size(axis))]
    )


def spread(values, masks, stack, row, frame):
    left = pltpu.roll(values, 1, 1) * masks[0]
    right = pltpu.roll(values, W - 1, 1) * masks[1]
    columns = slice(frame * W, (frame + 1) * W)
    for tap, shifted in enumerate((left, values, right)):
        start = row * TAPS + tap * C
        stack[start : start + C, columns] = shifted


def convolve(weights, stack, row, frames, sums):
    last = frames // 2
    for pair in range(last + 1):
        window = stack[row * TAPS : (row + 3) * TAPS, 2 * pair * W : (2 * pair + 2) * W]
        low, high = (0 if pair < last else 1), (3 if pair > 0 else 2)
        parts = jnp.dot(
            weights[low * C : high * C, :], window, preferred_element_type=jnp.float32
        )
        parts = {tap: parts[(tap - low) * C :][:C] for tap in range(low, high)}
        if 0 in parts:
            sums[row, :, 2 * pair * W : (2 * pair + 2) * W] = parts[0]
        for j in range(2):
            frame = 2 * pair + j - 1
            if 0 <= frame < frames:
                columns = slice(frame * W, (frame + 1) * W)
                sums[row, :, columns] = sums[row, :, columns] + parts[1][:, j * W : (j + 1) * W]
        if 2 in parts:
            yield 2 * pair - 2, sums[row, :, (2 * pair - 2) * W : 2 * pair * W] + parts[2]


def decode_kernel(joined, base, count, flags, gain_two, bias_one, bias_two, *rest):
    plain, raw, own, low, high = rest[:2], *rest[2:6]
    tails = rest[6:9]
    boxes, first, second, sums, done, weights_one, weights_two, stores = rest[-8:]

    @pl.when(flags[0] > 0)
    def _():
        lane = lax.broadcasted_iota(jnp.int32, (C, W), 1)
        masks = [
            jnp.where(lane == edge, 0.0, 1.0).astype(jnp.bfloat16) for edge in (0, W - 1)
        ]
        past = True if joined else flags[1] == 0
        above = flags[2] > 0
        below = flags[3] > 0
        zero = jnp.zeros((), jnp.bfloat16)
        lay_out(plain[0], weights_one)
        def fill(row):
            part, at = row // 2, row % 2
            side = {0: above, 2: below}.get(part)
            for frame in range(TAIL + count):
                place = base - TAIL + frame
                keep = None
                if place >= 0:
                    values = (low, own, high)[part][place, at]
                elif joined:
                    values = (low, own, high)[part][SEG + TAIL + place, at]
                else:
                    values = tails[part][TAIL + place, at]
                    keep = past
                if side is not None:
                    keep = side if keep is None else jnp.logical_and(keep, side)
                if keep is not None:
                    values = jnp.where(keep, values, zero)
                spread(values, masks, first, row, frame)

        gain = gain_two[...]
        offset_one = bias_one[...]
        offset_two = bias_two[...]

        def inner(row):
            for frame, total in convolve(weights_one, first, row, count + 2, sums):
                for j in range(2):
                    part = total[:, j * W : (j + 1) * W] + offset_one
                    part = part.astype(jnp.bfloat16).astype(jnp.float32)
                    part = activate(part, gain, 0)
                    keep = past if base + frame < 2 else None
                    side = {0: above, 3: below}.get(row)
                    if side is not None:
                        keep = side if keep is None else jnp.logical_and(keep, side)
                    if keep is not None:
                        part = jnp.where(keep, part, 0.0)
                    spread(part.astype(jnp.bfloat16), masks, second, row, frame + j)

        def store(block):
            return pltpu.make_async_copy(
                done.at[block], boxes.at[flags[5 + base // BF + block]], stores.at[block]
            )

        def outer(row):
            for start, total in convolve(weights_two, second, row, count, sums):
                for j in range(BF):
                    part = total[:, j * W : (j + 1) * W] + offset_two
                    part = part + raw[base + start + j, row].astype(jnp.float32)
                    part = jnp.where(base + start + j < flags[4], part, 0.0)
                    done[start // BF, j, row] = part.astype(jnp.bfloat16)
                if row == 1:
                    store(start // BF).start()

        for row in range(3):
            fill(row)
        inner(0)
        fill(3)
        inner(1)
        fill(4)
        lay_out(plain[1], weights_two)
        inner(2)
        fill(5)
        outer(0)
        inner(3)
        outer(1)
        for block in range(count // BF):
            store(block).wait()


def decode(part, flags, vectors, weights, raw, own, sides, tails, boxes, box_count):
    joined, base, count = part
    operands = [flags, *vectors, *weights, raw, own, *sides, *tails]
    specs = [pl.BlockSpec(memory_space=pltpu.SMEM)]
    specs += [pl.BlockSpec(memory_space=pltpu.VMEM)] * (len(operands) - 1)
    aliases = {}
    if boxes is not None:
        aliases = {len(operands): 0}
        operands.append(boxes)
        specs.append(pl.BlockSpec(memory_space=pl.ANY))
    taps = pltpu.VMEM((3 * C, 3 * TAPS), jnp.bfloat16)
    return pl.pallas_call(
        functools.partial(decode_kernel, joined, base, count),
        out_shape=jax.ShapeDtypeStruct((box_count, BF, 2, C, W), jnp.bfloat16),
        in_specs=specs,
        out_specs=pl.BlockSpec(memory_space=pl.ANY),
        scratch_shapes=[
            pltpu.VMEM((6 * TAPS, (TAIL + count) * W), jnp.bfloat16),
            pltpu.VMEM((4 * TAPS, (2 + count) * W), jnp.bfloat16),
            pltpu.VMEM((4, C, (2 + count) * W), jnp.float32),
            pltpu.VMEM((count // BF, BF, 2, C, W), jnp.bfloat16),
            taps,
            taps,
            pltpu.SemaphoreType.DMA((count // BF,)),
        ],
        input_output_aliases=aliases,
        compiler_params=pltpu.CompilerParams(vmem_limit_bytes=32 * 2**20),
        cost_estimate=pl.CostEstimate(flops=count * 750 * 10**6, bytes_accessed=4 * 10**6, transcendentals=0),
        name="decode",
    )(*operands)


def lay_out(weight, rows):
    for tap in range(3):
        for row in range(3):
            for cell in range(3):
                start = (row * 3 + cell) * C
                rows[tap * C : (tap + 1) * C, start : start + C] = weight[tap, row, cell]


def join_kernel(flags, own, last, past, low, high, joined):
    joined[:SEG] = own[...]

    @pl.when(flags[1] > 0)
    def _():
        joined[SEG:] = last[...]

    @pl.when(flags[1] == 0)
    def _():
        joined[SEG:] = past[...]


def join(flags, own, last, past, sides):
    operands = (flags, own, last, past, *sides)
    return pl.pallas_call(
        join_kernel,
        out_shape=jax.ShapeDtypeStruct((SEG + TAIL, 2, C, W), jnp.bfloat16),
        in_specs=[pl.BlockSpec(memory_space=pltpu.SMEM)]
        + [pl.BlockSpec(memory_space=pltpu.VMEM)] * (len(operands) - 1),
        out_specs=pl.BlockSpec(memory_space=pltpu.VMEM),
        compiler_params=pltpu.CompilerParams(vmem_limit_bytes=8 * 2**20),
        name="join",
    )(*operands)


def local(
    features, frame_counts, places, gain_one, gain_two, conv_one, conv_two, bias_one, bias_two
):
    my_video = lax.axis_index("video")
    my_tm = lax.axis_index("tm")
    my_height = lax.axis_index("height")
    videos = lax.axis_size("video")
    tm_count = lax.axis_size("tm")
    heights = lax.axis_size("height")
    rounds = features.shape[1]

    raw, own = [], []
    for turn in range(rounds):
        raw.append(jnp.swapaxes(features[0, turn], 1, 2))
        values = raw[turn].astype(jnp.float32)
        own.append(activate(values, gain_one[:, None], 2).astype(jnp.bfloat16))
    past_0, past_1 = (ring(value[SEG - TAIL :], "tm") for value in own)
    sides_0 = neighbours(own[0], "height")

    held = lax.dynamic_index_in_dim(
        places.reshape(videos, rounds, tm_count, RB), my_tm, 2, keepdims=False
    )
    mine = lax.dynamic_index_in_dim(held, my_video, 0, keepdims=False)
    count = lax.dynamic_index_in_dim(frame_counts, my_video, 0, keepdims=False)
    owner = mine // (SLOTS * tm_count)
    flags = []
    for turn in range(rounds):
        live = count > turn * tm_count * SEG
        leads = my_tm == 0
        limit = count - (turn * tm_count + my_tm) * SEG
        head = jnp.stack([live, leads, my_height > 0, my_height < heights - 1, limit])
        flags.append(jnp.concatenate([head, jnp.minimum(owner[turn], videos - 1)]).astype(jnp.int32))

    wide = [jnp.broadcast_to(v[:, None], (C, W)) for v in (gain_two, bias_one, bias_two)]
    weights = (conv_one, conv_two)
    wanted = (my_video * tm_count + my_tm) * SLOTS + jnp.arange(SLOTS)
    match = (held.reshape(videos, -1)[None] == wanted[:, None, None]).astype(jnp.int32)
    found = jnp.sum(match, axis=(1, 2)) > 0
    source = jnp.sum(match * jnp.arange(videos)[None, :, None], axis=(1, 2))

    past_0, flags, wide, found, source = lax.optimization_barrier(
        (past_0, flags, wide, found, source)
    )
    low_tail, high_tail = (ring(side[SEG - TAIL :], "tm") for side in sides_0)
    tails_0 = (low_tail, past_0, high_tail)
    joined = join(flags[1], own[1], past_0, past_1, sides_0)
    sides_1 = neighbours(joined, "height")
    boxes = None
    for part, turn, rows, sides, tails in (
        ((False, SEG // 2, SEG // 2), 0, own[0], sides_0, ()),
        ((False, 0, SEG // 2), 0, own[0], sides_0, tails_0),
        ((True, 0, SEG), 1, joined, sides_1, ()),
    ):
        boxes = decode(
            part, flags[turn], wide, weights, raw[turn], rows, sides, tails, boxes, videos
        )
    received = lax.all_to_all(boxes, "video", split_axis=0, concat_axis=0, tiled=True)
    chosen = jnp.take(received, source, axis=0, mode="clip")
    chosen = jnp.where(found[:, None, None, None, None], chosen, jnp.zeros((), jnp.bfloat16))
    return jnp.swapaxes(chosen, 2, 3).reshape(1, SLOTS * BF, C, 2, W)


def solution(mesh):
    placed = (P("video", None, "tm", None, "height", None), P(), P(), P(), P(), P(), P(), P(), P())
    return jax.shard_map(
        local,
        mesh=mesh,
        in_specs=placed,
        out_specs=P("video", "tm", None, "height", None),
        check_vma=False,
    )
```

```python
import functools

import jax
import jax.numpy as jnp
from jax import lax
from jax.experimental import pallas as pl
from jax.experimental.pallas import tpu as pltpu
from jax.sharding import PartitionSpec as P

EPS = 1e-06
BF = 2
RB = 4
SEG = BF * RB
TAIL = 2 * BF
C = 96
W = 128
TAPS = 3 * C
SLOTS = 5


def activate(values, gain, axis):
    mean_square = jnp.mean(values * values, axis=axis, keepdims=True)
    scaled = values * lax.rsqrt(mean_square + EPS) * gain
    return scaled * (0.5 * jnp.tanh(0.5 * scaled) + 0.5)


def ring(value, axis):
    count = lax.axis_size(axis)
    return lax.ppermute(value, axis, [(i, (i + 1) % count) for i in range(count)])


def neighbours(value, axis):
    return ring(value, axis), lax.ppermute(
        value, axis, [((i + 1) % lax.axis_size(axis), i) for i in range(lax.axis_size(axis))]
    )


def spread(values, masks, stack, row, frame):
    left = pltpu.roll(values, 1, 1) * masks[0]
    right = pltpu.roll(values, W - 1, 1) * masks[1]
    columns = slice(frame * W, (frame + 1) * W)
    for tap, shifted in enumerate((left, values, right)):
        start = row * TAPS + tap * C
        stack[start : start + C, columns] = shifted


def convolve(weights, stack, row, frames, sums):
    last = frames // 2
    for pair in range(last + 1):
        window = stack[row * TAPS : (row + 3) * TAPS, 2 * pair * W : (2 * pair + 2) * W]
        low, high = (0 if pair < last else 1), (3 if pair > 0 else 2)
        parts = jnp.dot(
            weights[low * C : high * C, :], window, preferred_element_type=jnp.float32
        )
        parts = {tap: parts[(tap - low) * C :][:C] for tap in range(low, high)}
        if 0 in parts:
            sums[row, :, 2 * pair * W : (2 * pair + 2) * W] = parts[0]
        for j in range(2):
            frame = 2 * pair + j - 1
            if 0 <= frame < frames:
                columns = slice(frame * W, (frame + 1) * W)
                sums[row, :, columns] = sums[row, :, columns] + parts[1][:, j * W : (j + 1) * W]
        if 2 in parts:
            yield 2 * pair - 2, sums[row, :, (2 * pair - 2) * W : 2 * pair * W] + parts[2]


def decode_kernel(joined, base, count, flags, gain_two, bias_one, bias_two, *rest):
    plain, raw, own, low, high = rest[:2], *rest[2:6]
    tails = rest[6:9]
    boxes, first, second, sums, done, weights_one, weights_two, stores = rest[-8:]

    @pl.when(flags[0] > 0)
    def _():
        lane = lax.broadcasted_iota(jnp.int32, (C, W), 1)
        masks = [
            jnp.where(lane == edge, 0.0, 1.0).astype(jnp.bfloat16) for edge in (0, W - 1)
        ]
        past = True if joined else flags[1] == 0
        above = flags[2] > 0
        below = flags[3] > 0
        zero = jnp.zeros((), jnp.bfloat16)
        lay_out(plain[0], weights_one)
        def fill(row):
            part, at = row // 2, row % 2
            side = {0: above, 2: below}.get(part)
            for frame in range(TAIL + count):
                place = base - TAIL + frame
                keep = None
                if place >= 0:
                    values = (low, own, high)[part][place, at]
                elif joined:
                    values = (low, own, high)[part][SEG + TAIL + place, at]
                else:
                    values = tails[part][TAIL + place, at]
                    keep = past
                if side is not None:
                    keep = side if keep is None else jnp.logical_and(keep, side)
                if keep is not None:
                    values = jnp.where(keep, values, zero)
                spread(values, masks, first, row, frame)

        gain = gain_two[...]
        offset_one = bias_one[...]
        offset_two = bias_two[...]

        def inner(row):
            for frame, total in convolve(weights_one, first, row, count + 2, sums):
                for j in range(2):
                    part = total[:, j * W : (j + 1) * W] + offset_one
                    part = part.astype(jnp.bfloat16).astype(jnp.float32)
                    part = activate(part, gain, 0)
                    keep = past if base + frame < 2 else None
                    side = {0: above, 3: below}.get(row)
                    if side is not None:
                        keep = side if keep is None else jnp.logical_and(keep, side)
                    if keep is not None:
                        part = jnp.where(keep, part, 0.0)
                    spread(part.astype(jnp.bfloat16), masks, second, row, frame + j)

        def store(block):
            return pltpu.make_async_copy(
                done.at[block], boxes.at[flags[5 + base // BF + block]], stores.at[block]
            )

        def outer(row):
            for start, total in convolve(weights_two, second, row, count, sums):
                for j in range(BF):
                    part = total[:, j * W : (j + 1) * W] + offset_two
                    part = part + raw[base + start + j, row].astype(jnp.float32)
                    part = jnp.where(base + start + j < flags[4], part, 0.0)
                    done[start // BF, j, row] = part.astype(jnp.bfloat16)
                if row == 1:
                    store(start // BF).start()

        for row in range(3):
            fill(row)
        inner(0)
        fill(3)
        inner(1)
        fill(4)
        lay_out(plain[1], weights_two)
        inner(2)
        fill(5)
        outer(0)
        inner(3)
        outer(1)
        for block in range(count // BF):
            store(block).wait()


def decode(part, flags, vectors, weights, raw, own, sides, tails, boxes, box_count):
    joined, base, count = part
    operands = [flags, *vectors, *weights, raw, own, *sides, *tails]
    specs = [pl.BlockSpec(memory_space=pltpu.SMEM)]
    specs += [pl.BlockSpec(memory_space=pltpu.VMEM)] * (len(operands) - 1)
    aliases = {}
    if boxes is not None:
        aliases = {len(operands): 0}
        operands.append(boxes)
        specs.append(pl.BlockSpec(memory_space=pl.ANY))
    taps = pltpu.VMEM((3 * C, 3 * TAPS), jnp.bfloat16)
    return pl.pallas_call(
        functools.partial(decode_kernel, joined, base, count),
        out_shape=jax.ShapeDtypeStruct((box_count, BF, 2, C, W), jnp.bfloat16),
        in_specs=specs,
        out_specs=pl.BlockSpec(memory_space=pl.ANY),
        scratch_shapes=[
            pltpu.VMEM((6 * TAPS, (TAIL + count) * W), jnp.bfloat16),
            pltpu.VMEM((4 * TAPS, (2 + count) * W), jnp.bfloat16),
            pltpu.VMEM((4, C, (2 + count) * W), jnp.float32),
            pltpu.VMEM((count // BF, BF, 2, C, W), jnp.bfloat16),
            taps,
            taps,
            pltpu.SemaphoreType.DMA((count // BF,)),
        ],
        input_output_aliases=aliases,
        compiler_params=pltpu.CompilerParams(vmem_limit_bytes=32 * 2**20),
        cost_estimate=pl.CostEstimate(flops=(12000 if base == 0 else 1) * 10**6, bytes_accessed=10**5, transcendentals=0),
        name="decode",
    )(*operands)


def lay_out(weight, rows):
    for tap in range(3):
        for row in range(3):
            for cell in range(3):
                start = (row * 3 + cell) * C
                rows[tap * C : (tap + 1) * C, start : start + C] = weight[tap, row, cell]


def join_kernel(flags, own, last, past, low, high, joined):
    joined[:SEG] = own[...]

    @pl.when(flags[1] > 0)
    def _():
        joined[SEG:] = last[...]

    @pl.when(flags[1] == 0)
    def _():
        joined[SEG:] = past[...]


def join(flags, own, last, past, sides):
    operands = (flags, own, last, past, *sides)
    return pl.pallas_call(
        join_kernel,
        out_shape=jax.ShapeDtypeStruct((SEG + TAIL, 2, C, W), jnp.bfloat16),
        in_specs=[pl.BlockSpec(memory_space=pltpu.SMEM)]
        + [pl.BlockSpec(memory_space=pltpu.VMEM)] * (len(operands) - 1),
        out_specs=pl.BlockSpec(memory_space=pltpu.VMEM),
        compiler_params=pltpu.CompilerParams(vmem_limit_bytes=8 * 2**20),
        name="join",
    )(*operands)


def local(
    features, frame_counts, places, gain_one, gain_two, conv_one, conv_two, bias_one, bias_two
):
    my_video = lax.axis_index("video")
    my_tm = lax.axis_index("tm")
    my_height = lax.axis_index("height")
    videos = lax.axis_size("video")
    tm_count = lax.axis_size("tm")
    heights = lax.axis_size("height")
    rounds = features.shape[1]

    raw, own = [], []
    for turn in range(rounds):
        raw.append(jnp.swapaxes(features[0, turn], 1, 2))
        values = raw[turn].astype(jnp.float32)
        own.append(activate(values, gain_one[:, None], 2).astype(jnp.bfloat16))
    past_0, past_1 = (ring(value[SEG - TAIL :], "tm") for value in own)
    sides_0 = neighbours(own[0], "height")

    held = lax.dynamic_index_in_dim(
        places.reshape(videos, rounds, tm_count, RB), my_tm, 2, keepdims=False
    )
    mine = lax.dynamic_index_in_dim(held, my_video, 0, keepdims=False)
    count = lax.dynamic_index_in_dim(frame_counts, my_video, 0, keepdims=False)
    owner = mine // (SLOTS * tm_count)
    flags = []
    for turn in range(rounds):
        live = count > turn * tm_count * SEG
        leads = my_tm == 0
        limit = count - (turn * tm_count + my_tm) * SEG
        head = jnp.stack([live, leads, my_height > 0, my_height < heights - 1, limit])
        flags.append(jnp.concatenate([head, jnp.minimum(owner[turn], videos - 1)]).astype(jnp.int32))

    wide = [jnp.broadcast_to(v[:, None], (C, W)) for v in (gain_two, bias_one, bias_two)]
    weights = (conv_one, conv_two)
    wanted = (my_video * tm_count + my_tm) * SLOTS + jnp.arange(SLOTS)
    match = (held.reshape(videos, -1)[None] == wanted[:, None, None]).astype(jnp.int32)
    found = jnp.sum(match, axis=(1, 2)) > 0
    source = jnp.sum(match * jnp.arange(videos)[None, :, None], axis=(1, 2))

    past_0, flags, wide, found, source = lax.optimization_barrier(
        (past_0, flags, wide, found, source)
    )
    beside = [side[SEG - TAIL :] for side in sides_0]
    low_tail, high_tail = (ring(side, "tm") for side in beside)
    tails_0 = (low_tail, past_0, high_tail)
    joined = join(flags[1], own[1], past_0, past_1, beside)
    sides_1 = neighbours(joined, "height")
    boxes = None
    for part, turn, rows, sides, tails in (
        ((False, SEG // 2, SEG // 2), 0, own[0], sides_0, ()),
        ((False, 0, SEG // 2), 0, own[0], sides_0, tails_0),
        ((True, 0, SEG), 1, joined, sides_1, ()),
    ):
        boxes = decode(
            part, flags[turn], wide, weights, raw[turn], rows, sides, tails, boxes, videos
        )
    received = lax.all_to_all(boxes, "video", split_axis=0, concat_axis=0, tiled=True)
    chosen = jnp.take(received, source, axis=0, mode="clip")
    chosen = jnp.where(found[:, None, None, None, None], chosen, jnp.zeros((), jnp.bfloat16))
    return jnp.swapaxes(chosen, 2, 3).reshape(1, SLOTS * BF, C, 2, W)


def solution(mesh):
    placed = (P("video", None, "tm", None, "height", None), P(), P(), P(), P(), P(), P(), P(), P())
    return jax.shard_map(
        local,
        mesh=mesh,
        in_specs=placed,
        out_specs=P("video", "tm", None, "height", None),
        check_vma=False,
    )
```
